256 devices in a mesh: grp: 8 (over y_lo, x), dom: 32 (over z, y_hi, core).
Axes of the slice: x: 4, y: 4 (y_hi: 2, y_lo: 2; y = y_hi * 2 + y_lo), z: 8, core: 2. Of those that a mesh axis runs over, the one named last changes fastest.
Arguments:
- positions: float32 [3, 16384], P(None, ('grp', 'dom')), may hold values from -6 to 6
- species: int32 [16384], P(('grp', 'dom')), may hold values from 0 to 7
- ghost_index: int32 [2048], P(('grp', 'dom')), may hold values from 0 to 63, as said below
- bin_load: int32 [256], P(('grp', 'dom')), may hold values from 2 to 16, as said below
- neighbour: int32 [4096, 256], P(('grp', 'dom')), may hold values from 0 to 95, as said below
- pair_count: int32 [4096, 4], P(('grp', 'dom')), may hold values from 32 to 64, as said below
- species_shift: float32 [8], replicated, may hold values from -4 to 4
- w_embed1: float32 [256, 24], replicated, may hold values from -5 to 5
- w_embed2: float32 [256, 256], replicated, may hold values from -0.375 to 0.375
- w_v0: float32 [64, 256], replicated, may hold values from -0.375 to 0.375
- w_env: float32 [2, 64, 256], replicated, may hold values from -0.375 to 0.375
- w_lat1: float32 [2, 256, 448], replicated, may hold values from -0.25 to 0.25
- w_lat2: float32 [2, 256, 256], replicated, may hold values from -0.375 to 0.375
- w_gate: float32 [1, 64, 256], replicated, may hold values from -0.375 to 0.375
- w_mix: float32 [1, 3, 64, 64], replicated, may hold values from -0.75 to 0.75
- w_out1: float32 [128, 256], replicated, may hold values from -0.375 to 0.375
- w_out2: float32 [128], replicated, may hold values from -0.5 to 0.5
Outputs:
- forces: float32 [3, 16384], P(None, ('grp', 'dom'))
- atom_energy: float32 [16384], P(('grp', 'dom'))
The draws below stay inside these ranges and needn't reach their ends.
Inputs may be any that keep to these rules, and one draw needn't show every extreme that they name: `ghost_index`: each device's list names 8 distinct atoms of its occupied bin slots. `bin_load`: the number of occupied bin slots of each device; occupied slots come first. `neighbour`: slots within a center's pair_count never name the center itself nor an own atom of an empty bin slot; other slots hold arbitrary valid indices. `pair_count`: occupied slots of a center are its first ones.
All inputs are finite; a program needn't handle non-finite values.
Results may differ from the reference program's by a relative error of at most 0.0003.
Values sent between devices are 32-bit elements; how exact they have to be, the bound alone decides.
No kernel may reach another device: no remote copies, remote signals or barrier semaphores. Data moves between devices by JAX's collectives and lax.ppermute only.
A program may use at most 128 MiB of HBM per device.

```python
import math
import jax
import jax.numpy as jnp
from jax import lax

CHAN = 64
LATENT = 256
EHID = 128
RADIAL = 8
SPECIES = 8
LAYERS = 2
NEIGH = 64
CENTERS = 4
BINS = 16
PAIRS = 256
ATOM_DEV = 64
GHOST = 8
EXTENDED = 96
ATOMS = 16384
SHELLS = 2048
BLOCKS = 4096
N_GRP = 8
N_DOM = 32


def shared_load(key):
    first, second = jax.random.split(jax.random.fold_in(key, 101))
    start = jax.random.randint(first, (N_GRP, 1), 0, N_DOM)
    place = jnp.arange(N_DOM)[None, :]
    inside = (place - start) % N_DOM < max(N_DOM // 4, 1)
    light = 2 + jax.random.randint(second, (N_GRP, N_DOM), 0, max(BINS // 2 - 1, 1))
    return jnp.where(inside, BINS, light).reshape(N_GRP * N_DOM).astype(jnp.int32)


def draw_bin_load(key, part):
    return shared_load(key)


def draw_ghost_index(key, part):
    load = shared_load(key)
    key = jax.random.fold_in(key, 5)
    live = (load * CENTERS)[:, None]
    drawn = jax.random.randint(key, (N_GRP * N_DOM, 1), 0, ATOM_DEV)
    start = jnp.where(load[:, None] == BINS, live - GHOST, drawn)
    return ((start + jnp.arange(GHOST)[None, :]) % live).reshape(SHELLS).astype(jnp.int32)


def draw_neighbour(key, part):
    load = shared_load(key)
    key = jax.random.fold_in(key, 7)
    first, second, third = jax.random.split(key, 3)
    live = jnp.repeat(load * CENTERS, BINS)[:, None]
    center = (jnp.arange(BLOCKS) % BINS)[:, None] * CENTERS + (jnp.arange(PAIRS) // NEIGH)[None, :]
    drawn = jax.random.randint(first, (BLOCKS, PAIRS), 0, 1 << 20) % (live - 1)
    owned = drawn + (drawn >= center).astype(jnp.int32)
    ghost = ATOM_DEV + jax.random.randint(second, (BLOCKS, PAIRS), 0, 4 * GHOST)
    chooser = jax.random.randint(third, (BLOCKS, PAIRS), 0, 2)
    return jnp.where(chooser == 1, ghost, owned).astype(jnp.int32)


def draw_pair_count(key, part):
    key = jax.random.fold_in(key, 9)
    counts = jax.random.randint(key, (BLOCKS, CENTERS), NEIGH // 2, NEIGH + 1)
    return counts.at[::BINS, 0].set(NEIGH).astype(jnp.int32)


def place_ends(array, key, smallest, largest):
    longest = array.shape.index(max(array.shape))
    spots = []
    for shift in (0, 1):
        where = [jax.random.randint(jax.random.fold_in(key, axis), (), 0, length) for axis, length in enumerate(array.shape)]
        where[longest] = (where[longest] + shift) % array.shape[longest]
        spots.append(tuple(where))
    return array.at[spots[0]].set(smallest).at[spots[1]].set(largest)


def level_of(own_key, extent, cuts, low, top_value):
    def one(axis_at, blocks):
        steps = jax.random.uniform(jax.random.fold_in(jax.random.fold_in(own_key, 6), axis_at), (blocks,), jnp.float32, low / len(cuts), top_value / len(cuts))
        return jnp.repeat(jnp.exp(steps), extent[axis_at] // blocks).reshape((-1,) + (1,) * (len(extent) - axis_at - 1))

    level = one(*cuts[0])
    for cut in cuts[1:]:
        level = level * one(*cut)
    return level


def gaussian(own_key, extent, scale, reach, cuts=(), held_as=jnp.bfloat16):
    values = scale * jax.random.normal(own_key, extent, jnp.float32)
    if cuts:
        values = values * level_of(own_key, extent, cuts, -0.22, 0.18)
    return jnp.clip(values, -reach, reach).astype(held_as)


def setup_inputs(seed: int = 0) -> dict:
    keys = jax.random.split(jax.random.key(seed), 18)
    positions = gaussian(keys[0], (3, ATOMS), 1.5, 6.0, ((1, 256),), jnp.float32)
    species = place_ends(jax.random.randint(keys[1], (ATOMS,), 0, SPECIES), jax.random.fold_in(keys[1], 1), 0, SPECIES - 1).astype(jnp.int32)
    ghost_index = draw_ghost_index(jax.random.fold_in(keys[17], 71), 0)
    bin_load = draw_bin_load(jax.random.fold_in(keys[17], 71), 0)
    neighbour = draw_neighbour(jax.random.fold_in(keys[17], 71), 0)
    pair_count = draw_pair_count(jax.random.fold_in(keys[17], 71), 0)
    species_shift = gaussian(keys[6], (SPECIES,), 1.0, 4.0, (), jnp.float32)
    w_embed1 = gaussian(keys[7], (LATENT, 2 * SPECIES + RADIAL), 1.0, 5.0, (), jnp.float32)
    w_embed2 = gaussian(keys[8], (LATENT, LATENT), LATENT ** -0.5, 0.375, (), jnp.float32)
    w_v0 = gaussian(keys[9], (CHAN, LATENT), LATENT ** -0.5, 0.375, (), jnp.float32)
    w_env = gaussian(keys[10], (LAYERS, CHAN, LATENT), LATENT ** -0.5, 0.375, (), jnp.float32)
    w_lat1 = gaussian(keys[11], (LAYERS, LATENT, LATENT + 3 * CHAN), (LATENT + 3 * CHAN) ** -0.5, 0.25, (), jnp.float32)
    w_lat2 = gaussian(keys[12], (LAYERS, LATENT, LATENT), LATENT ** -0.5, 0.375, (), jnp.float32)
    w_gate = gaussian(keys[13], (LAYERS - 1, CHAN, LATENT), LATENT ** -0.5, 0.375, (), jnp.float32)
    w_mix = gaussian(keys[14], (LAYERS - 1, 3, CHAN, CHAN), CHAN ** -0.5, 0.75, (), jnp.float32)
    w_out1 = gaussian(keys[15], (EHID, LATENT), LATENT ** -0.5, 0.375, (), jnp.float32)
    w_out2 = gaussian(keys[16], (EHID,), EHID ** -0.5, 0.5, (), jnp.float32)
    return dict(positions=positions, species=species, ghost_index=ghost_index, bin_load=bin_load, neighbour=neighbour, pair_count=pair_count, species_shift=species_shift, w_embed1=w_embed1, w_embed2=w_embed2, w_v0=w_v0, w_env=w_env, w_lat1=w_lat1, w_lat2=w_lat2, w_gate=w_gate, w_mix=w_mix, w_out1=w_out1, w_out2=w_out2)


highest = lax.Precision.HIGHEST
soft_sq = 0.25
basis_reach = 8.0
envelope_reach = 4.0
half_root = math.sqrt(0.5)

def matmul(left, right):
    return jnp.dot(left, right, precision=highest, preferred_element_type=jnp.float32)

def edge_geometry(offsets, radial):
    dist_sq = lax.optimization_barrier(jnp.sum(offsets * offsets, axis=0)) + soft_sq
    distance = jnp.sqrt(dist_sq)
    unit_x = offsets[0] / distance
    unit_y = offsets[1] / distance
    unit_z = offsets[2] / distance
    root3 = math.sqrt(3.0)
    root5 = math.sqrt(5.0)
    root15 = math.sqrt(15.0)
    harmonics = jnp.stack([jnp.ones_like(distance), root3 * unit_x, root3 * unit_y, root3 * unit_z, root15 * unit_x * unit_y, root15 * unit_y * unit_z, 0.5 * root5 * (2.0 * unit_z * unit_z - unit_x * unit_x - unit_y * unit_y), root15 * unit_x * unit_z, 0.5 * root15 * (unit_x * unit_x - unit_y * unit_y)])
    scaled = dist_sq / (envelope_reach * envelope_reach)
    envelope = 1.0 / (1.0 + scaled * scaled)
    orders = jnp.arange(1, radial + 1, dtype=jnp.float32)[:, None]
    basis = math.sqrt(2.0 / basis_reach) * jnp.sin(orders * (math.pi / basis_reach) * distance[None]) / distance[None] * envelope[None]
    return (harmonics, envelope, basis)

def two_body(offsets, kinds, embed_first, embed_second, tensor_weight):
    harmonics, envelope, basis = edge_geometry(offsets, embed_first.shape[1] - kinds.shape[0])
    inputs = jnp.concatenate([kinds, basis], axis=0)
    latent = envelope[None] * matmul(embed_second, jax.nn.silu(matmul(embed_first, inputs)))
    tensor = matmul(tensor_weight, latent)[None] * harmonics[:, None, :]
    return (latent, tensor, harmonics, envelope)

def interaction(latent, tensor, harmonics, envelope, valid, neigh, layer_weights):
    env_weight, lat_first, lat_second, gate_weight, mix_weight, out_first, out_second = layer_weights
    pairs = harmonics.shape[1]
    centers = pairs // neigh
    channels = env_weight.shape[1]
    layers = env_weight.shape[0]
    for layer in range(layers):
        weight = matmul(env_weight[layer], latent) * valid[None]
        spread = (harmonics[:, None, :] * weight[None]).reshape(9, channels, centers, neigh)
        gamma = lax.optimization_barrier(jnp.sum(spread, axis=3, keepdims=True)) * neigh ** (-0.5)
        gamma = jnp.broadcast_to(gamma, spread.shape).reshape(9, channels, pairs)
        product = tensor * gamma
        scalars = jnp.concatenate([product[0], lax.optimization_barrier(jnp.sum(product[1:4], axis=0)), lax.optimization_barrier(jnp.sum(product[4:9], axis=0))], axis=0)
        hidden = jax.nn.silu(matmul(lat_first[layer], jnp.concatenate([latent, scalars], axis=0)))
        latent = half_root * (latent + envelope[None] * matmul(lat_second[layer], hidden))
        if layer + 1 < layers:
            gate = matmul(gate_weight[layer], latent)
            tensor_zero = tensor[0]
            gamma_zero = gamma[0]
            coupled = tensor_zero[None] * gamma[1:] + gamma_zero[None] * tensor[1:]
            tensor_one = tensor[1:4]
            gamma_one = gamma[1:4]
            cross = jnp.stack([tensor_one[1] * gamma_one[2] - tensor_one[2] * gamma_one[1], tensor_one[2] * gamma_one[0] - tensor_one[0] * gamma_one[2], tensor_one[0] * gamma_one[1] - tensor_one[1] * gamma_one[0]])
            order_zero = (tensor_zero * gamma_zero * gate)[None]
            order_one = (coupled[0:3] + cross) * gate[None]
            order_two = coupled[3:8] * gate[None]
            mixed_zero = jnp.einsum('cd,mdp->mcp', mix_weight[layer, 0], order_zero, precision=highest)
            mixed_one = jnp.einsum('cd,mdp->mcp', mix_weight[layer, 1], order_one, precision=highest)
            mixed_two = jnp.einsum('cd,mdp->mcp', mix_weight[layer, 2], order_two, precision=highest)
            tensor = jnp.concatenate([mixed_zero, mixed_one, mixed_two], axis=0)
    edge = envelope * matmul(out_second[None], jax.nn.silu(matmul(out_first, latent)))[0]
    return lax.optimization_barrier(jnp.sum((edge * valid).reshape(centers, neigh), axis=1))

def beside_all(table, axis_grp, axis_dom):
    return [jnp.roll(table, 1, axis_grp), jnp.roll(table, -1, axis_grp), jnp.roll(table, 1, axis_dom), jnp.roll(table, -1, axis_dom)]

def reference(positions, species, ghost_index, bin_load, neighbour, pair_count, species_shift, w_embed1, w_embed2, w_v0, w_env, w_lat1, w_lat2, w_gate, w_mix, w_out1, w_out2):
    devices = N_GRP * N_DOM
    grid = positions.reshape(3, N_GRP, N_DOM, ATOM_DEV)
    kinds_grid = species.reshape(N_GRP, N_DOM, ATOM_DEV)
    shell_index = ghost_index.reshape(N_GRP, N_DOM, GHOST)
    shell_pos = jnp.take_along_axis(grid, shell_index[None], axis=3)
    shell_kind = jnp.take_along_axis(kinds_grid, shell_index, axis=2)
    owner = (jnp.arange(devices, dtype=jnp.int32) * ATOM_DEV).reshape(N_GRP, N_DOM, 1)
    own_global = owner + jnp.arange(ATOM_DEV, dtype=jnp.int32)[None, None]
    shell_global = owner + shell_index
    extended_pos = jnp.concatenate([grid] + beside_all(shell_pos, 1, 2), axis=3).reshape(3, devices, EXTENDED)
    extended_kind = jnp.concatenate([kinds_grid] + beside_all(shell_kind, 0, 1), axis=2).reshape(devices, EXTENDED)
    extended_global = jnp.concatenate([own_global] + beside_all(shell_global, 0, 1), axis=2).reshape(devices, EXTENDED)
    neighbour_flat = neighbour.reshape(devices, BINS * PAIRS)
    center_local = jnp.arange(BINS * PAIRS, dtype=jnp.int32) // NEIGH
    own_pos = grid.reshape(3, devices, ATOM_DEV)
    other_pos = jnp.take_along_axis(extended_pos, neighbour_flat[None], axis=2)
    center_pos = own_pos[:, :, center_local]
    offsets = jnp.transpose((other_pos - center_pos).reshape(3, BLOCKS, PAIRS), (1, 0, 2))
    center_kind = species.reshape(devices, ATOM_DEV)[:, center_local].reshape(BLOCKS, PAIRS)
    other_kind = jnp.take_along_axis(extended_kind, neighbour_flat, axis=1).reshape(BLOCKS, PAIRS)
    slot = jnp.arange(PAIRS, dtype=jnp.int32) % NEIGH
    valid = (slot[None] < jnp.repeat(pair_count, NEIGH, axis=1)).astype(jnp.float32)
    live = jnp.arange(BLOCKS, dtype=jnp.int32) % BINS < jnp.repeat(bin_load, BINS)
    layer_weights = (w_env, w_lat1, w_lat2, w_gate, w_mix, w_out1, w_out2)
    kind_range = jnp.arange(SPECIES, dtype=jnp.int32)[:, None]

    def one_block(item):
        offsets_one, center_one, other_one, valid_one, live_one = item

        def compute(operand):
            kinds = jnp.concatenate([center_one[None] == kind_range, other_one[None] == kind_range], axis=0).astype(jnp.float32)

            def energy_of(shifted):
                latent, tensor, harmonics, envelope = two_body(shifted, kinds, w_embed1, w_embed2, w_v0)
                return interaction(latent, tensor, harmonics, envelope, valid_one, NEIGH, layer_weights)
            energies, pull = jax.vjp(energy_of, offsets_one)
            return (energies, pull(jnp.ones_like(energies))[0])

        def skip(operand):
            return (jnp.zeros((CENTERS,), jnp.float32), jnp.zeros((3, PAIRS), jnp.float32))
        return lax.cond(live_one, compute, skip, 0)
    energies, grads = lax.map(one_block, (offsets, center_kind, other_kind, valid, live))
    center_force = lax.optimization_barrier(jnp.sum(grads.reshape(BLOCKS, 3, CENTERS, NEIGH), axis=3))
    forces = jnp.transpose(center_force, (1, 0, 2)).reshape(3, ATOMS)
    targets = jnp.take_along_axis(extended_global, neighbour_flat, axis=1).reshape(BLOCKS * PAIRS)
    forces = forces.at[:, targets].add(-jnp.transpose(grads, (1, 0, 2)).reshape(3, BLOCKS * PAIRS))
    live_atom = ((jnp.arange(ATOM_DEV, dtype=jnp.int32) // CENTERS)[None] < bin_load[:, None]).astype(jnp.float32).reshape(ATOMS)
    atom_energy = energies.reshape(ATOMS) + live_atom * species_shift[species]
    return (forces, atom_energy)
```

```python
import functools
import math

import jax
import jax.numpy as jnp
from jax import lax
from jax.experimental import pallas as pl
from jax.experimental.pallas import tpu as pltpu
from jax.sharding import PartitionSpec as P

f32 = jnp.float32
bf16 = jnp.bfloat16
highest = lax.Precision.HIGHEST
SEG = 256
SLOTS = 8
LANES = 128
CH = 64
ROOT3 = math.sqrt(3.0)
ROOT5 = math.sqrt(5.0)
ROOT15 = math.sqrt(15.0)
HALF = math.sqrt(0.5)
ORDER = (0, 1, 1, 1, 2, 2, 2, 2, 2)
Y_V, Y_W0, Y_Z2, Y_Q = 0, 64, 128, 384
Q_W1, Q_GATE, Q_Z3, Q_OUT = 0, 64, 128, 384
D_W1, D_GATE, D_Z3, D_OUT, D_Z2, D_V, D_W0 = 0, 192, 384, 1152, 1536, 2304, 2496
D_ALL = 2688


def dot(left, right):
    return lax.dot_general(left, right, (((1,), (0,)), ((), ())), preferred_element_type=f32)


def dot_nt(left, right):
    return lax.dot_general(left, right, (((1,), (1,)), ((), ())), preferred_element_type=f32)


def split(value):
    high = value.astype(bf16)
    return high, (value - high.astype(f32)).astype(bf16)


def put3(ref, base, count, row, lanes, value):
    high, low = split(value)
    rows = value.shape[0]
    ref[pl.ds(base + row, rows), lanes] = high
    ref[pl.ds(base + count + row, rows), lanes] = high
    ref[pl.ds(base + 2 * count + row, rows), lanes] = low


def put2(high_ref, low_ref, row, lanes, value):
    high, low = split(value)
    rows = value.shape[0]
    high_ref[pl.ds(row, rows), lanes] = high
    low_ref[pl.ds(row, rows), lanes] = low


def prepare_kernel(
    emb2, v0, env, lat1, lat2, gate, mix, out1,
    ca, c0, lb0, lb1, c1, mx, cat, c0t, lb0t, lb1t, c1t, mxt, full, tall,
):
    def mul(left, right):
        return jnp.dot(left, right, precision=highest, preferred_element_type=f32)

    def triple(value):
        high, low = split(value)
        return jnp.concatenate([high, low, high], axis=1)

    def triple_t(target, column, value):
        high = value.astype(bf16).astype(f32)
        low = (value - high).astype(bf16).astype(f32)
        rows = value.shape[0]
        tall[pl.ds(column, rows), :] = high
        tall[pl.ds(column + rows, rows), :] = low
        tall[pl.ds(column + 2 * rows, rows), :] = high

    def turn(target, rows):
        for at in range(0, rows, LANES):
            target[:, at : at + LANES] = jnp.transpose(tall[at : at + LANES, :]).astype(bf16)

    late = jnp.concatenate(
        [env[1] * (0.125 * HALF), gate[0] * HALF, lat1[1][:, :256] * HALF, out1[...] * (HALF * HALF)],
        axis=0,
    )
    early = jnp.concatenate([v0[...], env[0] * 0.125, lat1[0][:, :256]], axis=0)
    full[0:384] = mul(early, emb2[...])
    full[384:896] = mul(late, emb2[...])
    ca[...] = triple(full[...])
    for column, start, rows in (
        (D_W1, 384, 64), (D_GATE, 448, 64), (D_Z3, 512, 256), (D_OUT, 768, 128),
        (D_Z2, 128, 256), (D_V, 0, 64), (D_W0, 64, 64),
    ):
        triple_t(cat, column, full[start : start + rows])
    turn(cat, D_ALL)
    full[0:512] = mul(late, lat2[0])
    c0[...] = triple(full[0:512])
    for column, start, rows in ((D_W1, 0, 64), (D_GATE, 64, 64), (D_Z3, 128, 256), (D_OUT, 384, 128)):
        triple_t(c0t, column, full[start : start + rows])
    turn(c0t, 1536)
    full[0:128] = mul(out1[...] * HALF, lat2[1])
    c1[...] = triple(full[0:128])
    triple_t(c1t, 0, full[0:128])
    turn(c1t, 384)
    for layer, ahead, back in ((0, lb0, lb0t), (1, lb1, lb1t)):
        part = lat1[layer][:, 256:448]
        ahead[...] = triple(part)
        back[...] = triple(jnp.transpose(part))
    for order in range(3):
        mx[order] = triple(mix[0, order])
        mxt[order] = triple(jnp.transpose(mix[0, order]))


def prepare(emb2, v0, env, lat1, lat2, gate, mix, out1):
    shapes = [
        (896, 768), (512, 768), (256, 576), (256, 576), (128, 768), (3, 64, 192),
        (256, D_ALL), (256, 1536), (192, 768), (192, 768), (256, 384), (3, 64, 192),
    ]
    return pl.pallas_call(
        prepare_kernel,
        out_shape=[jax.ShapeDtypeStruct(s, bf16) for s in shapes],
        in_specs=[pl.BlockSpec(memory_space=pltpu.VMEM)] * 8,
        out_specs=[pl.BlockSpec(memory_space=pltpu.VMEM)] * len(shapes),
        scratch_shapes=[pltpu.VMEM((896, 256), f32), pltpu.VMEM((D_ALL, 256), f32)],
        compiler_params=pltpu.CompilerParams(vmem_limit_bytes=40 * 2**20),
        name="prepare",
    )(emb2, v0, env, lat1, lat2, gate, mix, out1)


def scratch_list(width):
    w, s = width, width // SEG
    return dict(
        oh=((256, w), bf16), sb=((256, w), bf16), sf=((SLOTS, w), f32), hb=((256, w), bf16),
        x1=((64, w), bf16), a=((768, w), bf16), s0=((576, w), bf16), b=((768, w), bf16),
        s1=((576, w), bf16), c=((768, w), bf16), dy=((D_ALL, w), bf16),
        u=((1728, w), bf16), dt=((1728, w), bf16), dg=((576, 2 * w), bf16),
        wh=((320, w), bf16), wl=((320, w), bf16),
        y=((896, w), f32), q=((512, w), f32),
        sa=((256, w), f32), da=((256, w), f32), sbb=((256, w), f32), dbb=((256, w), f32),
        sc=((256, w), f32), dc=((256, w), f32),
        a0=((192, w), f32), g0=((576, w), f32), g1=((576, w), f32), bm=((576, w), f32),
        t=((576, w), f32), du=((576, w), f32), vg=((64, w), f32), dv=((64, w), f32),
        gm=((2 * s, 64, LANES), f32), gd=((2 * s, 64, LANES), f32),
    )


NAMES = tuple(scratch_list(512))


class Stream:
    def __init__(self, refs, width):
        for name, ref in zip(NAMES, refs):
            setattr(self, name, ref)
        self.width = width
        self.segs = [slice(i * SEG, (i + 1) * SEG) for i in range(width // SEG)]
        self.all = slice(0, width)


def order_mask(order):
    lane = lax.broadcasted_iota(jnp.int32, (64, LANES), 1)
    low, high = ((0, 8), (8, 32), (32, 72))[order]
    return (lane >= low) & (lane < high)


def sublane_sum(value):
    return jnp.sum(value, axis=0, keepdims=True)


def fold(value):
    rows, lanes = value.shape
    return jnp.sum(value.reshape(rows // 8, 8, lanes), axis=0)


def pack(work, counts, tab, nbr, lanes, st, state):
    item, center = state
    owner = work[item, 0]
    last = work[item, 2]
    lane = lax.broadcasted_iota(jnp.int32, (1, SEG), 1)
    slot_row = lax.broadcasted_iota(jnp.int32, (SLOTS, SEG), 0)
    slot_lane = lax.broadcasted_iota(jnp.int32, (SLOTS, SEG), 1)
    inside = jnp.zeros((SLOTS, SEG), jnp.bool_)
    names = jnp.full((1, SEG), -1, jnp.int32)
    mine = jnp.full((1, SEG), -1, jnp.int32)
    filled = jnp.int32(0)
    going = jnp.bool_(True)
    taken = jnp.int32(0)
    for j in range(SLOTS):
        at = jnp.minimum(center + j, 63)
        count = counts[owner, at]
        going = going & (center + j < last) & (filled + count <= SEG)
        count = jnp.where(going, count, 0)
        row = nbr[pl.ds(owner * 64 + at, 1), :]
        row = jnp.concatenate([row, row], axis=1)
        row = pltpu.roll(row, filled, axis=1)
        here = (lane >= filled) & (lane < filled + count)
        names = jnp.where(here, row, names)
        mine = jnp.where(here, at, mine)
        inside = inside | (
            (slot_row == j) & (slot_lane >= filled) & (slot_lane < filled + count)
        )
        filled = filled + count
        taken = taken + going.astype(jnp.int32)
    seats = inside.astype(f32)
    st.sf[:, lanes] = seats
    both = jnp.concatenate([seats, jnp.zeros_like(seats)], axis=0).astype(bf16)
    st.sb[0:16, lanes] = both
    st.sb[128:144, lanes] = both
    for row in range(0, LANES, 32):
        atom = lax.broadcasted_iota(jnp.int32, (32, SEG), 0) + row
        st.oh[row : row + 32, lanes] = (atom == names).astype(f32).astype(bf16)
        st.oh[LANES + row : LANES + row + 32, lanes] = (atom == mine).astype(f32).astype(bf16)
    gathered = dot(tab[owner], st.oh[:, lanes])
    center = center + taken
    ended = center >= last
    item = jnp.where(ended, item + 1, item)
    center = jnp.where(ended, work[item, 1], center)
    return (item, center), owner, gathered


def spread(seg_gamma, seats):
    parts = [
        seg_gamma if m == 0 else pltpu.roll(seg_gamma, LANES - 8 * m, axis=1) for m in range(9)
    ]
    high, low = split(jnp.concatenate(parts, axis=0))
    return dot(jnp.concatenate([high, low], axis=1), seats)


def gather_gamma(parts):
    total = parts[0:64]
    for m in range(1, 9):
        total = total + pltpu.roll(parts[64 * m : 64 * m + 64], 8 * m, axis=1)
    return total


def with_harmonics(value, hb):
    high, low = split(value)
    return dot(jnp.concatenate([high, high], axis=1), hb) + dot(low, hb[0:LANES])


def over_harmonics(high, low, hb):
    first = dot_nt(high, hb)
    return first[:, :LANES] + first[:, LANES:] + dot_nt(low, hb[0:LANES])


def gate_curve(value):
    sig = 0.5 * jnp.tanh(0.5 * value) + 0.5
    act = value * sig
    return act, sig + act * (1.0 - sig)


def activate(st, product, base_ref, base_row, act_ref, slope_ref, target, env):
    for lanes in st.segs:
        scale = env[:, lanes]
        for row in range(0, 256, 32):
            value = product[row : row + 32, lanes]
            if base_ref is not None:
                value = value + base_ref[base_row + row : base_row + row + 32, lanes]
            act, slope = gate_curve(value)
            act_ref[row : row + 32, lanes] = act
            slope_ref[row : row + 32, lanes] = slope * scale
            put3(target, 0, 256, row, lanes, act * scale)


def deactivate(st, product, act_ref, slope_ref, target, base):
    sums = []
    for lanes in st.segs:
        total = jnp.zeros((8, SEG), f32)
        for row in range(0, 256, 32):
            value = product[row : row + 32, lanes]
            total = total + fold(value * act_ref[row : row + 32, lanes])
            put3(target, base, 256, row, lanes, value * slope_ref[row : row + 32, lanes])
        sums.append(sublane_sum(total))
    return jnp.concatenate(sums, axis=1)


def tile(st, w, work, counts, tab, nbr, out, state):
    ca, c0, lb0, lb1, c1, mx, cat, c0t, lb0t, lb1t, c1t, mxt, w1, e1t, w2 = w
    owners, gathered = [], []
    for lanes in st.segs:
        state, owner, got = pack(work, counts, tab, nbr, lanes, st, state)
        owners.append(owner)
        gathered.append(got)
    got = jnp.concatenate(gathered, axis=1) if len(gathered) > 1 else gathered[0]
    off = got[0:8] + got[8:16] + got[16:24]
    ox, oy, oz = off[0:1], off[1:2], off[2:3]
    st.x1[0:16, :] = got[24:40].astype(bf16)
    st.x1[16:32, :] = got[24:40].astype(bf16)
    dist_sq = ox * ox + oy * oy + oz * oz + 0.25
    dist = jnp.sqrt(dist_sq)
    inv = 1.0 / dist
    ux, uy, uz = ox * inv, oy * inv, oz * inv
    harm = [
        None, ROOT3 * ux, ROOT3 * uy, ROOT3 * uz, ROOT15 * ux * uy, ROOT15 * uy * uz,
        0.5 * ROOT5 * (2.0 * uz * uz - ux * ux - uy * uy), ROOT15 * ux * uz,
        0.5 * ROOT15 * (ux * ux - uy * uy),
    ]
    ratio = dist_sq * 0.0625
    env = 1.0 / (1.0 + ratio * ratio)
    angle = dist * (math.pi / 8.0)
    sin1, cos1 = jnp.sin(angle), jnp.cos(angle)
    sines, cosines = [sin1], [cos1]
    for _ in range(7):
        s, c = sines[-1], cosines[-1]
        sines.append(s * cos1 + c * sin1)
        cosines.append(c * cos1 - s * sin1)
    sines, cosines = jnp.concatenate(sines, axis=0), jnp.concatenate(cosines, axis=0)
    level = 0.5 * inv * env
    high = (sines * level).astype(bf16).astype(f32)
    pair = jnp.concatenate([high, sines * level - high], axis=0).astype(bf16)
    st.x1[32:48, :] = pair
    st.x1[48:64, :] = pair
    for lanes in st.segs:
        seats = st.sf[:, lanes]
        blocks = [seats] + [harm[m][:, lanes] * seats for m in range(1, 9)] + [jnp.zeros_like(seats)]
        for k in range(0, 10, 2):
            block = jnp.concatenate(blocks[k : k + 2], axis=0)
            h, l = split(block)
            st.hb[8 * k : 8 * k + 16, lanes] = h
            st.hb[LANES + 8 * k : LANES + 8 * k + 16, lanes] = l
    activate(st, dot(w1[...], st.x1[...]), None, 0, st.sa, st.da, st.a, env)
    st.y[...] = dot(ca[...], st.a[...])
    for i, lanes in enumerate(st.segs):
        put2(st.wh, st.wl, 64, lanes, st.y[Y_W0 : Y_W0 + 64, lanes])
        hb = st.hb[:, lanes]
        gamma = over_harmonics(st.wh[64:128, lanes], st.wl[64:128, lanes], hb)
        st.gm[i] = gamma
        masked = jnp.concatenate([jnp.where(order_mask(l), gamma, 0.0) for l in range(3)], axis=0)
        scale = with_harmonics(masked, hb)
        st.a0[:, lanes] = scale
        for row in range(0, 192, 32):
            value = st.y[Y_V + row % 64 : Y_V + row % 64 + 32, lanes]
            put3(st.s0, 0, 192, row, lanes, value * scale[row : row + 32])
    activate(st, dot(lb0[...], st.s0[...]), st.y, Y_Z2, st.sbb, st.dbb, st.b, env)
    st.q[...] = dot(c0[...], st.b[...]) + st.y[Y_Q : Y_Q + 512, :]
    for i, lanes in enumerate(st.segs):
        st.g0[:, lanes] = spread(st.gm[i], st.sb[:, lanes])
        put2(st.wh, st.wl, 0, lanes, st.q[Q_W1 : Q_W1 + 64, lanes])
        hb = st.hb[:, lanes]
        gamma = over_harmonics(st.wh[0:64, lanes], st.wl[0:64, lanes], hb)
        st.gm[len(st.segs) + i] = gamma
        st.g1[:, lanes] = spread(gamma, st.sb[:, lanes])
    for lanes in st.segs:
        h = [None] + [harm[m][:, lanes] for m in range(1, 9)]
        for row in range(0, 64, 16):
            vg = st.y[Y_V + row : Y_V + row + 16, lanes] * st.q[Q_GATE + row : Q_GATE + row + 16, lanes]
            st.vg[row : row + 16, lanes] = vg
            g = [st.g0[64 * m + row : 64 * m + row + 16, lanes] for m in range(9)]
            mixed = [g[0]] + [g[m] + g[0] * h[m] for m in range(1, 9)]
            mixed[1] = mixed[1] + (h[2] * g[3] - h[3] * g[2])
            mixed[2] = mixed[2] + (h[3] * g[1] - h[1] * g[3])
            mixed[3] = mixed[3] + (h[1] * g[2] - h[2] * g[1])
            for m in range(9):
                st.bm[64 * m + row : 64 * m + row + 16, lanes] = mixed[m]
                put3(st.u, 192 * m, 64, row, lanes, vg * mixed[m])
    for m in range(9):
        st.t[64 * m : 64 * m + 64, :] = dot(mx[ORDER[m]], st.u[192 * m : 192 * m + 192, :])
    for lanes in st.segs:
        for row in range(0, 64, 16):
            total = [None, None, None]
            for m in range(9):
                at = slice(64 * m + row, 64 * m + row + 16)
                term = st.t[at, lanes] * st.g1[at, lanes]
                o = ORDER[m]
                total[o] = term if total[o] is None else total[o] + term
            for o in range(3):
                put3(st.s1, 0, 192, 64 * o + row, lanes, total[o])
    activate(st, dot(lb1[...], st.s1[...]), st.q, Q_Z3, st.sc, st.dc, st.c, env)
    final = dot(c1[...], st.c[...])
    valid = sublane_sum(st.sf[...])
    reads = []
    for lanes in st.segs:
        total = jnp.zeros((8, SEG), f32)
        scale = env[:, lanes] * valid[:, lanes]
        for row in range(0, 128, 32):
            value = final[row : row + 32, lanes] + st.q[Q_OUT + row : Q_OUT + row + 32, lanes]
            act, slope = gate_curve(value)
            weight = w2[row : row + 32, :]
            weight = jnp.concatenate([weight, weight], axis=1)
            total = total + fold(act * weight)
            put3(st.dy, D_OUT, 128, row, lanes, slope * weight * scale)
        reads.append(sublane_sum(total))
    read = jnp.concatenate(reads, axis=1) * valid
    energy = read * env
    d_env = deactivate(st, dot(c1t[...], st.dy[D_OUT : D_OUT + 384, :]), st.sc, st.dc, st.dy, D_Z3)
    d_scal = dot(lb1t[...], st.dy[D_Z3 : D_Z3 + 768, :])
    for i, lanes in enumerate(st.segs):
        for row in range(0, 64, 16):
            for m in range(9):
                at = slice(64 * m + row, 64 * m + row + 16)
                part = d_scal[64 * ORDER[m] + row : 64 * ORDER[m] + row + 16, lanes]
                put3(st.dt, 192 * m, 64, row, lanes, st.g1[at, lanes] * part)
                high, low = split(st.t[at, lanes] * part)
                st.dg[at, 2 * SEG * i : 2 * SEG * i + SEG] = high
                st.dg[at, 2 * SEG * i + SEG : 2 * SEG * i + 2 * SEG] = low
    for i, lanes in enumerate(st.segs):
        seats = st.sb[0:LANES, lanes]
        seats = jnp.concatenate([seats, seats], axis=1)
        d_gamma = gather_gamma(dot_nt(st.dg[:, 2 * SEG * i : 2 * SEG * i + 2 * SEG], seats))
        st.gd[len(st.segs) + i] = d_gamma
        d_weight = with_harmonics(d_gamma, st.hb[:, lanes])
        put3(st.dy, D_W1, 64, 0, lanes, d_weight)
    for m in range(9):
        st.du[64 * m : 64 * m + 64, :] = dot(mxt[ORDER[m]], st.dt[192 * m : 192 * m + 192, :])
    d_harm = []
    for i, lanes in enumerate(st.segs):
        h = [None] + [harm[m][:, lanes] for m in range(1, 9)]
        sums = [jnp.zeros((8, SEG), f32) for _ in range(8)]
        for row in range(0, 64, 16):
            rows = slice(row, row + 16)
            vg = st.vg[rows, lanes]
            d_vg = jnp.zeros((16, SEG), f32)
            d = []
            for m in range(9):
                at = slice(64 * m + row, 64 * m + row + 16)
                grad = st.du[at, lanes]
                d_vg = d_vg + grad * st.bm[at, lanes]
                d.append(grad * vg)
            value = st.y[Y_V + row : Y_V + row + 16, lanes]
            gate = st.q[Q_GATE + row : Q_GATE + row + 16, lanes]
            put3(st.dy, D_GATE, 64, row, lanes, value * d_vg)
            st.dv[rows, lanes] = gate * d_vg
            g = [st.g0[64 * m + row : 64 * m + row + 16, lanes] for m in range(4)]
            terms = [g[0] * d[m] for m in range(1, 9)]
            terms[0] = terms[0] + (g[2] * d[3] - g[3] * d[2])
            terms[1] = terms[1] + (g[3] * d[1] - g[1] * d[3])
            terms[2] = terms[2] + (g[1] * d[2] - g[2] * d[1])
            sums = [a + fold(b) for a, b in zip(sums, terms)]
            first = d[0]
            for m in range(1, 9):
                first = first + h[m] * d[m]
            back = [first] + d[1:]
            back[1] = back[1] + (h[3] * d[2] - h[2] * d[3])
            back[2] = back[2] + (h[1] * d[3] - h[3] * d[1])
            back[3] = back[3] + (h[2] * d[1] - h[1] * d[2])
            for m in range(9):
                at = slice(64 * m + row, 64 * m + row + 16)
                high, low = split(back[m])
                st.dg[at, 2 * SEG * i : 2 * SEG * i + SEG] = high
                st.dg[at, 2 * SEG * i + SEG : 2 * SEG * i + 2 * SEG] = low
        d_harm.append([sublane_sum(x) for x in sums])
    d_env = d_env + deactivate(st, dot(c0t[...], st.dy[0:1536, :]), st.sbb, st.dbb, st.dy, D_Z2)
    d_scal = dot(lb0t[...], st.dy[D_Z2 : D_Z2 + 768, :])
    for i, lanes in enumerate(st.segs):
        for row in range(0, 64, 32):
            rows = slice(row, row + 32)
            value = st.y[Y_V + row : Y_V + row + 32, lanes]
            d_value = st.dv[rows, lanes]
            for o in range(3):
                at = slice(64 * o + row, 64 * o + row + 32)
                part = d_scal[at, lanes]
                d_value = d_value + part * st.a0[at, lanes]
                put2(st.wh, st.wl, 128 + 64 * o + row, lanes, value * part)
            put3(st.dy, D_V, 64, row, lanes, d_value)
        hb = st.hb[:, lanes]
        seats = st.sb[0:LANES, lanes]
        seats = jnp.concatenate([seats, seats], axis=1)
        d_gamma = gather_gamma(dot_nt(st.dg[:, 2 * SEG * i : 2 * SEG * i + 2 * SEG], seats))
        d_scale = over_harmonics(st.wh[128:320, lanes], st.wl[128:320, lanes], hb)
        for o in range(3):
            d_gamma = d_gamma + jnp.where(order_mask(o), d_scale[64 * o : 64 * o + 64], 0.0)
        put3(st.dy, D_W0, 64, 0, lanes, with_harmonics(d_gamma, hb))
        gamma = st.gm[i]
        left = [st.gd[len(st.segs) + i], d_gamma]
        left = left + [jnp.where(order_mask(l), gamma, 0.0) for l in range(3)]
        left = jnp.concatenate([jnp.transpose(x) for x in (
            jnp.concatenate(left[0:2], axis=0), jnp.concatenate(left[2:4], axis=0),
            jnp.concatenate([left[4], jnp.zeros((64, LANES), f32)], axis=0),
        )], axis=1)
        high, low = split(left[0:80])
        high, low = high[:, 0:320], low[:, 0:320]
        d_seated = (
            dot(high, st.wh[:, lanes]) + dot(low, st.wh[:, lanes]) + dot(high, st.wl[:, lanes])
        )
        seats = st.sf[:, lanes]
        for m in range(1, 9):
            d_harm[i][m - 1] = d_harm[i][m - 1] + sublane_sum(d_seated[8 * m : 8 * m + 8] * seats)
    d_env = d_env + deactivate(st, dot(cat[...], st.dy[...]), st.sa, st.da, st.a, 0)
    d_basis = dot(e1t[...], st.a[...])[0:8]
    d_env = d_env + read
    dh = [None] + [jnp.concatenate([x[m] for x in d_harm], axis=1) for m in range(8)]
    dux = ROOT3 * dh[1] + ROOT15 * (uy * dh[4] + uz * dh[7] + ux * dh[8]) - ROOT5 * ux * dh[6]
    duy = ROOT3 * dh[2] + ROOT15 * (ux * dh[4] + uz * dh[5] - uy * dh[8]) - ROOT5 * uy * dh[6]
    duz = ROOT3 * dh[3] + ROOT15 * (uy * dh[5] + ux * dh[7]) + 2.0 * ROOT5 * uz * dh[6]
    order = (lax.broadcasted_iota(jnp.int32, (8, st.width), 0) + 1).astype(f32)
    sine_part = sublane_sum(sines * d_basis)
    cos_part = sublane_sum(order * cosines * d_basis)
    d_env = d_env + 0.5 * inv * sine_part
    d_inv = 0.5 * env * sine_part + ox * dux + oy * duy + oz * duz
    d_dist = (math.pi / 8.0) * level * cos_part
    d_sq = -0.125 * ratio * env * env * d_env + 0.5 * inv * d_dist - 0.5 * inv * inv * inv * d_inv
    d_sq = 2.0 * d_sq
    grad = [inv * dux + d_sq * ox, inv * duy + d_sq * oy, inv * duz + d_sq * oz]
    rows = jnp.concatenate(grad + [energy, jnp.zeros((4, st.width), f32)], axis=0)
    row_id = lax.broadcasted_iota(jnp.int32, (8, LANES), 0)
    for i, lanes in enumerate(st.segs):
        high = rows[:, lanes].astype(bf16).astype(f32)
        low = rows[:, lanes] - high
        sent = dot_nt(jnp.concatenate([high, low], axis=0).astype(bf16), st.oh[:, lanes])
        sent = sent[0:8] + sent[8:16]
        other, own = sent[:, :LANES], sent[:, LANES:]
        out[owners[i]] = out[owners[i]] + jnp.where(row_id < 3, own - other, own)
    return state


def force_kernel(width, owners, work, counts, ext, nbr, *rest):
    weights, out = rest[:15], rest[15]
    tab, scratch = rest[16], rest[17:]
    st = Stream(scratch, width)
    out[...] = jnp.zeros_like(out)
    st.sb[...] = jnp.zeros_like(st.sb)
    st.hb[...] = jnp.zeros_like(st.hb)
    kind = lax.broadcasted_iota(jnp.int32, (8, LANES), 0).astype(f32)
    row = lax.broadcasted_iota(jnp.int32, (8, LANES), 0)
    for owner in range(owners):
        value = ext[owner]
        place = jnp.where(row < 3, value, 0.0)
        high = place.astype(bf16).astype(f32)
        rest_of = place - high
        mid = rest_of.astype(bf16).astype(f32)
        low = (rest_of - mid).astype(bf16).astype(f32)
        named = (kind == value[3:4]).astype(f32)
        none = jnp.zeros_like(named)
        first = jnp.concatenate([high, mid, low, none, named, none], axis=0)
        second = jnp.concatenate([-high, -mid, -low, named, none, none], axis=0)
        tab[owner] = jnp.concatenate([first, second], axis=1).astype(bf16)
    total = work[4, 0]

    def step(state):
        return tile(st, weights, work, counts, tab, nbr, out, state)

    lax.while_loop(lambda s: s[0] < total, step, (jnp.int32(0), work[0, 1]))


def run_forces(work, counts, ext, nbr, weights, width=512):
    owners = ext.shape[0]
    scratch = scratch_list(width)
    vmem = pl.BlockSpec(memory_space=pltpu.VMEM)
    smem = pl.BlockSpec(memory_space=pltpu.SMEM)
    return pl.pallas_call(
        functools.partial(force_kernel, width, owners),
        out_shape=jax.ShapeDtypeStruct((owners, 8, LANES), f32),
        in_specs=[smem, smem, vmem, vmem] + [vmem] * len(weights),
        out_specs=vmem,
        scratch_shapes=[pltpu.VMEM((owners, 48, 256), bf16)]
        + [pltpu.VMEM(shape, kind) for shape, kind in scratch.values()],
        compiler_params=pltpu.CompilerParams(vmem_limit_bytes=52 * 2**20),
        name="forces",
    )(work, counts, ext, nbr, *weights)


def all_weights(w_embed1, w_embed2, w_v0, w_env, w_lat1, w_lat2, w_gate, w_mix, w_out1, w_out2):
    prepared = prepare(w_embed2, w_v0, w_env, w_lat1, w_lat2, w_gate, w_mix, w_out1)
    high = lax.reduce_precision(w_embed1, 8, 7)
    low = w_embed1 - high
    kinds = w_embed1.shape[1] - 8
    kh, kl, bh, bl = high[:, :kinds], low[:, :kinds], high[:, kinds:], low[:, kinds:]
    first = jnp.concatenate([kh, kl, bh, bh, bl, bl], axis=1).astype(bf16)
    back = jnp.concatenate([bh.T, bl.T, bh.T], axis=1)
    back = jnp.pad(back, ((0, 8), (0, 0))).astype(bf16)
    wide = jnp.broadcast_to(w_out2[:, None], (w_out2.shape[0], LANES))
    return tuple(prepared) + (first, back, wide)


def beside(cells, axis, step):
    count = lax.axis_size(axis)
    return lax.ppermute(cells, axis, [(i, (i + step) % count) for i in range(count)])


def local(
    positions,
    species,
    ghost_index,
    bin_load,
    neighbour,
    pair_count,
    species_shift,
    w_embed1,
    w_embed2,
    w_v0,
    w_env,
    w_lat1,
    w_lat2,
    w_gate,
    w_mix,
    w_out1,
    w_out2,
):
    atoms = positions.shape[1]
    bins, pairs = neighbour.shape
    centers = pair_count.shape[1]
    ghosts = ghost_index.shape[0]
    load = bin_load[0]
    named = ghost_index[:, None] == jnp.arange(atoms)[None, :]
    whole = jnp.concatenate([positions, species.astype(f32)[None]], axis=0)
    shell = jnp.sum(jnp.where(named[None], whole[:, None, :], 0.0), axis=2)
    received = [beside(shell, "grp", 1), beside(shell, "grp", -1), beside(shell, "dom", 1), beside(shell, "dom", -1)]
    weights = all_weights(
        w_embed1, w_embed2, w_v0, w_env, w_lat1, w_lat2, w_gate, w_mix, w_out1, w_out2
    )
    ext = jnp.concatenate([whole] + received, axis=1)
    ext = jnp.pad(ext, ((0, 4), (0, LANES - ext.shape[1])))[None]
    names = jnp.pad(neighbour.reshape(bins * centers, pairs // centers), ((0, 0), (0, 64)))
    counts = pair_count.reshape(1, bins * centers)
    end = load * centers
    zero = jnp.int32(0)
    row = jnp.stack([zero, zero, end, zero])
    work = jnp.zeros((8, 4), jnp.int32).at[0].set(row).at[4, 0].set(1)
    result = run_forces(work, counts, ext, names, weights)[0]
    energies = result[3, :atoms]
    force = result[0:3, :atoms]
    ghost = result[0:3, atoms : atoms + 4 * ghosts].reshape(3, 4, ghosts)
    back = (
        beside(ghost[:, 0], "grp", -1)
        + beside(ghost[:, 1], "grp", 1)
        + beside(ghost[:, 2], "dom", -1)
        + beside(ghost[:, 3], "dom", 1)
    )
    forces = force + jnp.sum(jnp.where(named[None], back[:, :, None], 0.0), axis=1)
    live = jnp.arange(atoms) // centers < load
    kind_range = jnp.arange(species_shift.shape[0])
    shift = jnp.sum(
        jnp.where(species[:, None] == kind_range[None], species_shift[None, :], 0.0), axis=1
    )
    return (forces, energies + jnp.where(live, shift, 0.0))


def solution(mesh):
    spread_over = ("grp", "dom")
    in_specs = (
        P(None, spread_over),
        P(spread_over),
        P(spread_over),
        P(spread_over),
        P(spread_over, None),
        P(spread_over, None),
    ) + (P(),) * 11
    out_specs = (P(None, spread_over), P(spread_over))
    return jax.shard_map(local, mesh=mesh, in_specs=in_specs, out_specs=out_specs, check_vma=False)
```

```python
import functools
import itertools
import math

import jax
import jax.numpy as jnp
from jax import lax
from jax.experimental import pallas as pl
from jax.experimental.pallas import tpu as pltpu
from jax.sharding import PartitionSpec as P

f32 = jnp.float32
bf16 = jnp.bfloat16
highest = lax.Precision.HIGHEST
SEG = 256
BIN_ROWS = 16
FORCES_MIB = 60
SLOTS = 8
LANES = 128
CH = 64
ROOT3 = math.sqrt(3.0)
ROOT5 = math.sqrt(5.0)
ROOT15 = math.sqrt(15.0)
HALF = math.sqrt(0.5)
ORDER = (0, 1, 1, 1, 2, 2, 2, 2, 2)
Y_V, Y_W0, Y_Z2, Y_Q = 0, 64, 128, 384
Q_W1, Q_GATE, Q_Z3, Q_OUT = 0, 64, 128, 384
D_W1, D_GATE, D_Z3, D_OUT, D_Z2, D_V, D_W0 = 0, 192, 384, 1152, 1536, 2304, 2496
D_ALL = 2688


def dot(left, right):
    return lax.dot_general(left, right, (((1,), (0,)), ((), ())), preferred_element_type=f32)


def dot_nt(left, right):
    return lax.dot_general(left, right, (((1,), (1,)), ((), ())), preferred_element_type=f32)


def split(value):
    high = value.astype(bf16)
    return high, (value - high.astype(f32)).astype(bf16)


def put3(ref, base, count, row, lanes, value):
    high, low = split(value)
    rows = value.shape[0]
    ref[pl.ds(base + row, rows), lanes] = high
    ref[pl.ds(base + count + row, rows), lanes] = high
    ref[pl.ds(base + 2 * count + row, rows), lanes] = low


def put2(high_ref, low_ref, row, lanes, value):
    high, low = split(value)
    rows = value.shape[0]
    high_ref[pl.ds(row, rows), lanes] = high
    low_ref[pl.ds(row, rows), lanes] = low


RAW_SHAPES = (
    (24, 256), (256, 256), (64, 256), (2, 64, 256), (2, 448, 256), (2, 256, 256), (1, 64, 256),
    (1, 3, 64, 64), (128, 256), (1, 128),
)
READY_SHAPES = (
    (896, 768), (512, 768), (256, 576), (256, 576), (128, 768), (3, 64, 192),
    (256, D_ALL), (256, 1536), (192, 768), (192, 768), (256, 384), (3, 64, 192),
    (256, 64), (16, 768),
)


def prepare_weights(raw, ready, full, tall):
    emb1, emb2, v0, env, lat1, lat2, gate, mix, out1, out2 = raw
    ca, c0, lb0, lb1, c1, mx, cat, c0t, lb0t, lb1t, c1t, mxt, w1, e1t, wide = ready

    def mul(left, right):
        return jnp.dot(left, right, precision=highest, preferred_element_type=f32)

    def triple(value):
        high, low = split(value)
        return jnp.concatenate([high, low, high], axis=1)

    def triple_t(target, column, value):
        high = value.astype(bf16).astype(f32)
        low = (value - high).astype(bf16).astype(f32)
        rows = value.shape[0]
        tall[pl.ds(column, rows), :] = high
        tall[pl.ds(column + rows, rows), :] = low
        tall[pl.ds(column + 2 * rows, rows), :] = high

    def turn(target, rows):
        for at in range(0, rows, LANES):
            target[:, at : at + LANES] = jnp.transpose(tall[at : at + LANES, :]).astype(bf16)

    kinds_h, kinds_l = (x.astype(f32) for x in split(emb1[0:16]))
    basis_h, basis_l = (x.astype(f32) for x in split(emb1[16:24]))
    tall[0:LANES] = jnp.concatenate(
        [kinds_h, kinds_l, basis_h, basis_h, basis_l, basis_l, jnp.zeros((64, 256), f32)], axis=0
    )
    w1[...] = jnp.transpose(tall[0:LANES]).astype(bf16)[:, 0:64]
    e1t[...] = jnp.concatenate(
        [jnp.concatenate([basis_h, basis_l, basis_h], axis=1), jnp.zeros((8, 768), f32)], axis=0
    ).astype(bf16)
    wide[...] = jnp.transpose(jnp.broadcast_to(out2[...], (LANES, LANES)))
    lat1_a = [jnp.transpose(lat1[layer, 0:256]) for layer in range(2)]
    late = jnp.concatenate(
        [env[1] * (0.125 * HALF), gate[0] * HALF, lat1_a[1] * HALF, out1[...] * (HALF * HALF)],
        axis=0,
    )
    early = jnp.concatenate([v0[...], env[0] * 0.125, lat1_a[0]], axis=0)
    full[0:384] = mul(early, emb2[...])
    full[384:896] = mul(late, emb2[...])
    ca[...] = triple(full[...])
    for column, start, rows in (
        (D_W1, 384, 64), (D_GATE, 448, 64), (D_Z3, 512, 256), (D_OUT, 768, 128),
        (D_Z2, 128, 256), (D_V, 0, 64), (D_W0, 64, 64),
    ):
        triple_t(cat, column, full[start : start + rows])
    turn(cat, D_ALL)
    full[0:512] = mul(late, lat2[0])
    c0[...] = triple(full[0:512])
    for column, start, rows in ((D_W1, 0, 64), (D_GATE, 64, 64), (D_Z3, 128, 256), (D_OUT, 384, 128)):
        triple_t(c0t, column, full[start : start + rows])
    turn(c0t, 1536)
    full[0:128] = mul(out1[...] * HALF, lat2[1])
    c1[...] = triple(full[0:128])
    triple_t(c1t, 0, full[0:128])
    turn(c1t, 384)
    for layer, ahead, back in ((0, lb0, lb0t), (1, lb1, lb1t)):
        part = lat1[layer, 256:448]
        ahead[...] = triple(jnp.transpose(part))
        back[...] = triple(part)
    for order in range(3):
        mx[order] = triple(mix[0, order])
        mxt[order] = triple(jnp.transpose(mix[0, order]))


def scratch_list(width):
    w, s = width, width // SEG
    return dict(
        oh=((256, w), bf16), sb=((256, w), bf16), sf=((SLOTS, w), f32), hb=((256, w), bf16),
        x1=((64, w), bf16), a=((768, w), bf16), s0=((576, w), bf16), dy=((D_ALL, w), bf16),
        u=((1728, w), bf16), dg=((576, 2 * w), bf16),
        wh=((320, w), bf16), wl=((320, w), bf16),
        y=((896, w), f32), q=((512, w), f32),
        sa=((256, w), f32), da=((256, w), f32), sbb=((256, w), f32), dbb=((256, w), f32),
        sc=((256, w), f32), dc=((256, w), f32),
        a0=((192, w), f32), g0=((576, w), f32), g1=((576, w), f32), bm=((576, w), f32),
        t=((576, w), f32), vg=((64, w), f32), dv=((64, w), f32),
        gm=((2 * s, 64, LANES), f32), gd=((2 * s, 64, LANES), f32),
    )


NAMES = tuple(scratch_list(512))


class Stream:
    def __init__(self, refs, width):
        for name, ref in zip(NAMES, refs):
            setattr(self, name, ref)
        self.b = self.c = self.a
        self.s1, self.dt, self.du = self.s0, self.u, self.g1
        self.width = width
        self.segs = [slice(i * SEG, (i + 1) * SEG) for i in range(width // SEG)]
        self.all = slice(0, width)


def order_mask(order):
    lane = lax.broadcasted_iota(jnp.int32, (64, LANES), 1)
    low, high = ((0, 8), (8, 32), (32, 72))[order]
    return (lane >= low) & (lane < high)


def sublane_sum(value):
    return jnp.sum(value, axis=0, keepdims=True)


def fold(value):
    rows, lanes = value.shape
    return jnp.sum(value.reshape(rows // 8, 8, lanes), axis=0)


def pack(work, tab, names_ref, lanes, st, state):
    item, center = state
    owner = jnp.minimum(item, 1)
    last = jnp.where(item == 0, work.own_end, work.other_end)
    last = jnp.where(item > 1, 0, last)
    lane = lax.broadcasted_iota(jnp.int32, (1, SEG), 1)
    slot_row = lax.broadcasted_iota(jnp.int32, (SLOTS, SEG), 0)
    slot_lane = lax.broadcasted_iota(jnp.int32, (SLOTS, SEG), 1)
    inside = jnp.zeros((SLOTS, SEG), jnp.bool_)
    names = jnp.full((1, SEG), -1, jnp.int32)
    mine = jnp.full((1, SEG), -1, jnp.int32)
    filled = jnp.int32(0)
    going = jnp.bool_(True)
    taken = jnp.int32(0)
    for j in range(SLOTS):
        at = jnp.minimum(center + j, 63)
        bin_at, part = lax.shift_right_logical(at, 2), at & 3
        count = jnp.where(owner == 0, work.own[part, bin_at], work.other[part, bin_at])
        going = going & (center + j < last) & (filled + count <= SEG)
        count = jnp.where(going, count, 0)
        row = names_ref[pl.ds(owner * BIN_ROWS + bin_at, 1), :]
        row = pltpu.roll(row, (filled + SEG - 64 * part) & (SEG - 1), axis=1)
        here = (lane >= filled) & (lane < filled + count)
        names = jnp.where(here, row, names)
        mine = jnp.where(here, at, mine)
        inside = inside | (
            (slot_row == j) & (slot_lane >= filled) & (slot_lane < filled + count)
        )
        filled = filled + count
        taken = taken + going.astype(jnp.int32)
    seats = inside.astype(f32)
    st.sf[:, lanes] = seats
    both = jnp.concatenate([seats, jnp.zeros_like(seats)], axis=0).astype(bf16)
    st.sb[0:16, lanes] = both
    st.sb[128:144, lanes] = both
    for row in range(0, LANES, 32):
        atom = lax.broadcasted_iota(jnp.int32, (32, SEG), 0) + row
        st.oh[row : row + 32, lanes] = (atom == names).astype(f32).astype(bf16)
        st.oh[LANES + row : LANES + row + 32, lanes] = (atom == mine).astype(f32).astype(bf16)
    gathered = dot(tab[owner], st.oh[:, lanes])
    center = center + taken
    ended = center >= last
    center = jnp.where(ended & (item == 0), work.other_start, center)
    item = jnp.where(ended, jnp.minimum(item + 1, 2), item)
    return (item, center), owner, gathered


def spread(seg_gamma, seats):
    parts = [
        seg_gamma if m == 0 else pltpu.roll(seg_gamma, LANES - 8 * m, axis=1) for m in range(9)
    ]
    high, low = split(jnp.concatenate(parts, axis=0))
    return dot(jnp.concatenate([high, low], axis=1), seats)


def gather_gamma(parts):
    total = parts[0:64]
    for m in range(1, 9):
        total = total + pltpu.roll(parts[64 * m : 64 * m + 64], 8 * m, axis=1)
    return total


def with_harmonics(value, hb):
    high, low = split(value)
    return dot(jnp.concatenate([high, high], axis=1), hb) + dot(low, hb[0:LANES])


def over_harmonics(high, low, hb):
    first = dot_nt(high, hb)
    return first[:, :LANES] + first[:, LANES:] + dot_nt(low, hb[0:LANES])


def gate_curve(value):
    sig = 0.5 * jnp.tanh(0.5 * value) + 0.5
    act = value * sig
    return act, sig + act * (1.0 - sig)


def activate(st, product, base_ref, base_row, act_ref, slope_ref, target, env):
    for lanes in st.segs:
        scale = env[:, lanes]
        for row in range(0, 256, 32):
            value = product[row : row + 32, lanes]
            if base_ref is not None:
                value = value + base_ref[base_row + row : base_row + row + 32, lanes]
            act, slope = gate_curve(value)
            act_ref[row : row + 32, lanes] = act
            slope_ref[row : row + 32, lanes] = slope * scale
            put3(target, 0, 256, row, lanes, act * scale)


def deactivate(st, product, act_ref, slope_ref, target, base):
    sums = []
    for lanes in st.segs:
        total = jnp.zeros((8, SEG), f32)
        for row in range(0, 256, 32):
            value = product[row : row + 32, lanes]
            total = total + fold(value * act_ref[row : row + 32, lanes])
            put3(target, base, 256, row, lanes, value * slope_ref[row : row + 32, lanes])
        sums.append(sublane_sum(total))
    return jnp.concatenate(sums, axis=1)


def fill(st, work, tab, names_ref, state):
    owners, gathered = [], []
    for lanes in st.segs:
        state, owner, got = pack(work, tab, names_ref, lanes, st, state)
        owners.append(owner)
        gathered.append(got)
    got = jnp.concatenate(gathered, axis=1) if len(gathered) > 1 else gathered[0]
    return state, owners, got


def tile(st, w, owners, got, out):
    ca, c0, lb0, lb1, c1, mx, cat, c0t, lb0t, lb1t, c1t, mxt, w1, e1t, w2 = w
    off = got[0:8] + got[8:16] + got[16:24]
    ox, oy, oz = off[0:1], off[1:2], off[2:3]
    st.x1[0:16, :] = got[24:40].astype(bf16)
    st.x1[16:32, :] = got[24:40].astype(bf16)
    dist_sq = ox * ox + oy * oy + oz * oz + 0.25
    dist = jnp.sqrt(dist_sq)
    inv = 1.0 / dist
    ux, uy, uz = ox * inv, oy * inv, oz * inv
    harm = [
        None, ROOT3 * ux, ROOT3 * uy, ROOT3 * uz, ROOT15 * ux * uy, ROOT15 * uy * uz,
        0.5 * ROOT5 * (2.0 * uz * uz - ux * ux - uy * uy), ROOT15 * ux * uz,
        0.5 * ROOT15 * (ux * ux - uy * uy),
    ]
    ratio = dist_sq * 0.0625
    env = 1.0 / (1.0 + ratio * ratio)
    angle = dist * (math.pi / 8.0)
    sin1, cos1 = jnp.sin(angle), jnp.cos(angle)
    sines, cosines = [sin1], [cos1]
    for _ in range(7):
        s, c = sines[-1], cosines[-1]
        sines.append(s * cos1 + c * sin1)
        cosines.append(c * cos1 - s * sin1)
    sines, cosines = jnp.concatenate(sines, axis=0), jnp.concatenate(cosines, axis=0)
    level = 0.5 * inv * env
    high = (sines * level).astype(bf16).astype(f32)
    pair = jnp.concatenate([high, sines * level - high], axis=0).astype(bf16)
    st.x1[32:48, :] = pair
    st.x1[48:64, :] = pair
    for lanes in st.segs:
        seats = st.sf[:, lanes]
        blocks = [seats] + [harm[m][:, lanes] * seats for m in range(1, 9)] + [jnp.zeros_like(seats)]
        for k in range(0, 10, 2):
            block = jnp.concatenate(blocks[k : k + 2], axis=0)
            h, l = split(block)
            st.hb[8 * k : 8 * k + 16, lanes] = h
            st.hb[LANES + 8 * k : LANES + 8 * k + 16, lanes] = l
    yield
    activate(st, dot(w1[...], st.x1[...]), None, 0, st.sa, st.da, st.a, env)
    yield
    st.y[...] = dot(ca[...], st.a[...])
    yield
    for i, lanes in enumerate(st.segs):
        put2(st.wh, st.wl, 64, lanes, st.y[Y_W0 : Y_W0 + 64, lanes])
        hb = st.hb[:, lanes]
        gamma = over_harmonics(st.wh[64:128, lanes], st.wl[64:128, lanes], hb)
        st.gm[i] = gamma
        masked = jnp.concatenate([jnp.where(order_mask(l), gamma, 0.0) for l in range(3)], axis=0)
        scale = with_harmonics(masked, hb)
        st.a0[:, lanes] = scale
        for row in range(0, 192, 32):
            value = st.y[Y_V + row % 64 : Y_V + row % 64 + 32, lanes]
            put3(st.s0, 0, 192, row, lanes, value * scale[row : row + 32])
    yield
    activate(st, dot(lb0[...], st.s0[...]), st.y, Y_Z2, st.sbb, st.dbb, st.b, env)
    yield
    st.q[...] = dot(c0[...], st.b[...]) + st.y[Y_Q : Y_Q + 512, :]
    yield
    for i, lanes in enumerate(st.segs):
        st.g0[:, lanes] = spread(st.gm[i], st.sb[:, lanes])
        put2(st.wh, st.wl, 0, lanes, st.q[Q_W1 : Q_W1 + 64, lanes])
        hb = st.hb[:, lanes]
        gamma = over_harmonics(st.wh[0:64, lanes], st.wl[0:64, lanes], hb)
        st.gm[len(st.segs) + i] = gamma
        st.g1[:, lanes] = spread(gamma, st.sb[:, lanes])
    yield
    for lanes in st.segs:
        h = [None] + [harm[m][:, lanes] for m in range(1, 9)]
        for row in range(0, 64, 16):
            vg = st.y[Y_V + row : Y_V + row + 16, lanes] * st.q[Q_GATE + row : Q_GATE + row + 16, lanes]
            st.vg[row : row + 16, lanes] = vg
            g = [st.g0[64 * m + row : 64 * m + row + 16, lanes] for m in range(9)]
            mixed = [g[0]] + [g[m] + g[0] * h[m] for m in range(1, 9)]
            mixed[1] = mixed[1] + (h[2] * g[3] - h[3] * g[2])
            mixed[2] = mixed[2] + (h[3] * g[1] - h[1] * g[3])
            mixed[3] = mixed[3] + (h[1] * g[2] - h[2] * g[1])
            for m in range(9):
                st.bm[64 * m + row : 64 * m + row + 16, lanes] = mixed[m]
                put3(st.u, 192 * m, 64, row, lanes, vg * mixed[m])
    yield
    for m in range(9):
        st.t[64 * m : 64 * m + 64, :] = dot(mx[ORDER[m]], st.u[192 * m : 192 * m + 192, :])
    yield
    for lanes in st.segs:
        for row in range(0, 64, 16):
            total = [None, None, None]
            for m in range(9):
                at = slice(64 * m + row, 64 * m + row + 16)
                term = st.t[at, lanes] * st.g1[at, lanes]
                o = ORDER[m]
                total[o] = term if total[o] is None else total[o] + term
            for o in range(3):
                put3(st.s1, 0, 192, 64 * o + row, lanes, total[o])
    yield
    activate(st, dot(lb1[...], st.s1[...]), st.q, Q_Z3, st.sc, st.dc, st.c, env)
    yield
    final = dot(c1[...], st.c[...])
    valid = sublane_sum(st.sf[...])
    reads = []
    for lanes in st.segs:
        total = jnp.zeros((8, SEG), f32)
        scale = env[:, lanes] * valid[:, lanes]
        for row in range(0, 128, 32):
            value = final[row : row + 32, lanes] + st.q[Q_OUT + row : Q_OUT + row + 32, lanes]
            act, slope = gate_curve(value)
            weight = w2[row : row + 32, :]
            weight = jnp.concatenate([weight, weight], axis=1)
            total = total + fold(act * weight)
            put3(st.dy, D_OUT, 128, row, lanes, slope * weight * scale)
        reads.append(sublane_sum(total))
    read = jnp.concatenate(reads, axis=1) * valid
    energy = read * env
    yield
    d_env = deactivate(st, dot(c1t[...], st.dy[D_OUT : D_OUT + 384, :]), st.sc, st.dc, st.dy, D_Z3)
    yield
    d_scal = dot(lb1t[...], st.dy[D_Z3 : D_Z3 + 768, :])
    yield
    for i, lanes in enumerate(st.segs):
        for row in range(0, 64, 16):
            for m in range(9):
                at = slice(64 * m + row, 64 * m + row + 16)
                part = d_scal[64 * ORDER[m] + row : 64 * ORDER[m] + row + 16, lanes]
                put3(st.dt, 192 * m, 64, row, lanes, st.g1[at, lanes] * part)
                high, low = split(st.t[at, lanes] * part)
                st.dg[at, 2 * SEG * i : 2 * SEG * i + SEG] = high
                st.dg[at, 2 * SEG * i + SEG : 2 * SEG * i + 2 * SEG] = low
    yield
    for i, lanes in enumerate(st.segs):
        seats = st.sb[0:LANES, lanes]
        seats = jnp.concatenate([seats, seats], axis=1)
        d_gamma = gather_gamma(dot_nt(st.dg[:, 2 * SEG * i : 2 * SEG * i + 2 * SEG], seats))
        st.gd[len(st.segs) + i] = d_gamma
        d_weight = with_harmonics(d_gamma, st.hb[:, lanes])
        put3(st.dy, D_W1, 64, 0, lanes, d_weight)
    yield
    for m in range(9):
        st.du[64 * m : 64 * m + 64, :] = dot(mxt[ORDER[m]], st.dt[192 * m : 192 * m + 192, :])
    yield
    d_harm = []
    for i, lanes in enumerate(st.segs):
        h = [None] + [harm[m][:, lanes] for m in range(1, 9)]
        sums = [jnp.zeros((8, SEG), f32) for _ in range(8)]
        for row in range(0, 64, 16):
            rows = slice(row, row + 16)
            vg = st.vg[rows, lanes]
            d_vg = jnp.zeros((16, SEG), f32)
            d = []
            for m in range(9):
                at = slice(64 * m + row, 64 * m + row + 16)
                grad = st.du[at, lanes]
                d_vg = d_vg + grad * st.bm[at, lanes]
                d.append(grad * vg)
            value = st.y[Y_V + row : Y_V + row + 16, lanes]
            gate = st.q[Q_GATE + row : Q_GATE + row + 16, lanes]
            put3(st.dy, D_GATE, 64, row, lanes, value * d_vg)
            st.dv[rows, lanes] = gate * d_vg
            g = [st.g0[64 * m + row : 64 * m + row + 16, lanes] for m in range(4)]
            terms = [g[0] * d[m] for m in range(1, 9)]
            terms[0] = terms[0] + (g[2] * d[3] - g[3] * d[2])
            terms[1] = terms[1] + (g[3] * d[1] - g[1] * d[3])
            terms[2] = terms[2] + (g[1] * d[2] - g[2] * d[1])
            sums = [a + fold(b) for a, b in zip(sums, terms)]
            first = d[0]
            for m in range(1, 9):
                first = first + h[m] * d[m]
            back = [first] + d[1:]
            back[1] = back[1] + (h[3] * d[2] - h[2] * d[3])
            back[2] = back[2] + (h[1] * d[3] - h[3] * d[1])
            back[3] = back[3] + (h[2] * d[1] - h[1] * d[2])
            for m in range(9):
                at = slice(64 * m + row, 64 * m + row + 16)
                high, low = split(back[m])
                st.dg[at, 2 * SEG * i : 2 * SEG * i + SEG] = high
                st.dg[at, 2 * SEG * i + SEG : 2 * SEG * i + 2 * SEG] = low
        d_harm.append([sublane_sum(x) for x in sums])
    yield
    d_env = d_env + deactivate(st, dot(c0t[...], st.dy[0:1536, :]), st.sbb, st.dbb, st.dy, D_Z2)
    yield
    d_scal = dot(lb0t[...], st.dy[D_Z2 : D_Z2 + 768, :])
    yield
    for i, lanes in enumerate(st.segs):
        for row in range(0, 64, 32):
            rows = slice(row, row + 32)
            value = st.y[Y_V + row : Y_V + row + 32, lanes]
            d_value = st.dv[rows, lanes]
            for o in range(3):
                at = slice(64 * o + row, 64 * o + row + 32)
                part = d_scal[at, lanes]
                d_value = d_value + part * st.a0[at, lanes]
                put2(st.wh, st.wl, 128 + 64 * o + row, lanes, value * part)
            put3(st.dy, D_V, 64, row, lanes, d_value)
        hb = st.hb[:, lanes]
        seats = st.sb[0:LANES, lanes]
        seats = jnp.concatenate([seats, seats], axis=1)
        d_gamma = gather_gamma(dot_nt(st.dg[:, 2 * SEG * i : 2 * SEG * i + 2 * SEG], seats))
        d_scale = over_harmonics(st.wh[128:320, lanes], st.wl[128:320, lanes], hb)
        for o in range(3):
            d_gamma = d_gamma + jnp.where(order_mask(o), d_scale[64 * o : 64 * o + 64], 0.0)
        put3(st.dy, D_W0, 64, 0, lanes, with_harmonics(d_gamma, hb))
        gamma = st.gm[i]
        left = [st.gd[len(st.segs) + i], d_gamma]
        left = left + [jnp.where(order_mask(l), gamma, 0.0) for l in range(3)]
        left = jnp.concatenate([jnp.transpose(x) for x in (
            jnp.concatenate(left[0:2], axis=0), jnp.concatenate(left[2:4], axis=0),
            jnp.concatenate([left[4], jnp.zeros((64, LANES), f32)], axis=0),
        )], axis=1)
        high, low = split(left[0:80])
        high, low = high[:, 0:320], low[:, 0:320]
        d_seated = (
            dot(high, st.wh[:, lanes]) + dot(low, st.wh[:, lanes]) + dot(high, st.wl[:, lanes])
        )
        seats = st.sf[:, lanes]
        for m in range(1, 9):
            d_harm[i][m - 1] = d_harm[i][m - 1] + sublane_sum(d_seated[8 * m : 8 * m + 8] * seats)
    yield
    d_env = d_env + deactivate(st, dot(cat[...], st.dy[...]), st.sa, st.da, st.a, 0)
    d_basis = dot(e1t[...], st.a[...])[0:8]
    d_env = d_env + read
    yield
    dh = [None] + [jnp.concatenate([x[m] for x in d_harm], axis=1) for m in range(8)]
    dux = ROOT3 * dh[1] + ROOT15 * (uy * dh[4] + uz * dh[7] + ux * dh[8]) - ROOT5 * ux * dh[6]
    duy = ROOT3 * dh[2] + ROOT15 * (ux * dh[4] + uz * dh[5] - uy * dh[8]) - ROOT5 * uy * dh[6]
    duz = ROOT3 * dh[3] + ROOT15 * (uy * dh[5] + ux * dh[7]) + 2.0 * ROOT5 * uz * dh[6]
    order = (lax.broadcasted_iota(jnp.int32, (8, st.width), 0) + 1).astype(f32)
    sine_part = sublane_sum(sines * d_basis)
    cos_part = sublane_sum(order * cosines * d_basis)
    d_env = d_env + 0.5 * inv * sine_part
    d_inv = 0.5 * env * sine_part + ox * dux + oy * duy + oz * duz
    d_dist = (math.pi / 8.0) * level * cos_part
    d_sq = -0.125 * ratio * env * env * d_env + 0.5 * inv * d_dist - 0.5 * inv * inv * inv * d_inv
    d_sq = 2.0 * d_sq
    grad = [inv * dux + d_sq * ox, inv * duy + d_sq * oy, inv * duz + d_sq * oz]
    rows = jnp.concatenate(grad + [energy, jnp.zeros((4, st.width), f32)], axis=0)
    row_id = lax.broadcasted_iota(jnp.int32, (8, LANES), 0)
    for i, lanes in enumerate(st.segs):
        high = rows[:, lanes].astype(bf16).astype(f32)
        low = rows[:, lanes] - high
        sent = dot_nt(jnp.concatenate([high, low], axis=0).astype(bf16), st.oh[:, lanes])
        sent = sent[0:8] + sent[8:16]
        other, own = sent[:, :LANES], sent[:, LANES:]
        out[owners[i]] = out[owners[i]] + jnp.where(row_id < 3, own - other, own)


class Work:
    pass


def force_kernel(width, load, own_counts, other_load, other_counts, mine, other, nbr, *rest):
    sources, out, tab, names_ref = rest[:10], rest[10], rest[11], rest[12]
    raw, weights, full, tall, sems = rest[13:23], rest[23:38], rest[38], rest[39], rest[40]
    scratch = rest[41:]
    copies = [
        pltpu.make_async_copy(source, target, sems.at[i])
        for i, (source, target) in enumerate(zip(sources, raw))
    ]
    for copy in copies:
        copy.start()
    each = len(NAMES)
    streams = [
        Stream(scratch[i : i + each], width) for i in range(0, len(scratch), each)
    ]
    out[...] = jnp.zeros_like(out)
    for st in streams:
        st.sb[...] = jnp.zeros_like(st.sb)
        st.hb[...] = jnp.zeros_like(st.hb)
    names_ref[0:16, :] = nbr[...]
    names_ref[16:24, :] = jnp.zeros((8, SEG), jnp.int32)
    names_ref[24:32, :] = other[8:16, :].astype(jnp.int32)
    kind = lax.broadcasted_iota(jnp.int32, (8, LANES), 0).astype(f32)
    row = lax.broadcasted_iota(jnp.int32, (8, LANES), 0)
    lane = lax.broadcasted_iota(jnp.int32, (8, LANES), 1)
    for owner, source in enumerate((mine, other)):
        value = jnp.where(lane < 96, source[0:8, 0:LANES], 0.0)
        place = jnp.where(row < 3, value, 0.0)
        high = place.astype(bf16).astype(f32)
        rest_of = place - high
        mid = rest_of.astype(bf16).astype(f32)
        low = (rest_of - mid).astype(bf16).astype(f32)
        named = (kind == value[3:4]).astype(f32)
        none = jnp.zeros_like(named)
        first = jnp.concatenate([high, mid, low, none, named, none], axis=0)
        second = jnp.concatenate([-high, -mid, -low, named, none, none], axis=0)
        tab[owner] = jnp.concatenate([first, second], axis=1).astype(bf16)
    work = Work()
    work.own, work.other = own_counts, other_counts
    own_all, other_all = load[0] * 4, other_load[0] * 4
    share = jnp.maximum(2 * (load[0] + other_load[0]), 32)
    work.own_end = jnp.minimum(own_all, share)
    work.other_start = jnp.minimum(other_all, share)
    work.other_end = other_all
    total = jnp.where(work.other_start < other_all, 2, 1)
    for copy in copies:
        copy.wait()
    prepare_weights(raw, weights, full, tall)

    def step(state):
        runs = []
        for st in streams:
            state, owners, got = fill(st, work, tab, names_ref, state)
            runs.append(tile(st, weights, owners, got, out))
        for _ in itertools.zip_longest(*runs):
            pass
        return state

    lax.while_loop(lambda s: s[0] < total, step, (jnp.int32(0), jnp.int32(0)))


def run_forces(load, own_counts, other_load, other_counts, mine, other, nbr, weights, width=1024, streams=1):
    scratch = scratch_list(width)
    vmem = pl.BlockSpec(memory_space=pltpu.VMEM)
    smem = pl.BlockSpec(memory_space=pltpu.SMEM)
    return pl.pallas_call(
        functools.partial(force_kernel, width),
        out_shape=jax.ShapeDtypeStruct((2, 8, LANES), f32),
        in_specs=[smem] * 4 + [vmem] * 3 + [pl.BlockSpec(memory_space=pl.ANY)] * len(weights),
        out_specs=vmem,
        scratch_shapes=[pltpu.VMEM((2, 48, 256), bf16), pltpu.VMEM((32, SEG), jnp.int32)]
        + [pltpu.VMEM(shape, f32) for shape in RAW_SHAPES]
        + [pltpu.VMEM(shape, bf16) for shape in READY_SHAPES]
        + [pltpu.VMEM((128, LANES), f32), pltpu.VMEM((896, 256), f32)]
        + [pltpu.VMEM((D_ALL, 256), f32), pltpu.SemaphoreType.DMA((len(weights),))]
        + [pltpu.VMEM(shape, kind) for shape, kind in list(scratch.values()) * streams],
        compiler_params=pltpu.CompilerParams(vmem_limit_bytes=FORCES_MIB * 2**20),
        name="forces",
    )(load, own_counts, other_load, other_counts, mine, other, nbr, *weights)


def shell_kernel(ghost, place, kind, out):
    lane = lax.broadcasted_iota(jnp.int32, (8, 64), 1)
    whole = jnp.concatenate([place[...], kind[...].astype(f32), jnp.zeros((4, 64), f32)], axis=0)
    spot = lax.broadcasted_iota(jnp.int32, (8, 8), 1)
    total = jnp.zeros((8, 8), f32)
    for k in range(8):
        one = jnp.sum(jnp.where(lane == ghost[k], whole, 0.0), axis=1, keepdims=True)
        total = total + jnp.where(spot == k, one, 0.0)
    out[...] = total[0:4]


def shell_of(ghost, place, kind):
    vmem = pl.BlockSpec(memory_space=pltpu.VMEM)
    return pl.pallas_call(
        shell_kernel,
        out_shape=jax.ShapeDtypeStruct((4, 8), f32),
        in_specs=[pl.BlockSpec(memory_space=pltpu.SMEM), vmem, vmem],
        out_specs=vmem,
        name="shell",
    )(ghost, place, kind[None])


def payload_kernel(load, place, kind, first, second, third, fourth, counts, nbr, out):
    whole = jnp.concatenate([place[...], kind[...].astype(f32)], axis=0)
    top = jnp.concatenate(
        [whole, first[...], second[...], third[...], fourth[...], jnp.zeros((4, 160), f32)], axis=1
    )
    loads = jnp.zeros((4, 1), jnp.int32) + load[0]
    low = jnp.concatenate(
        [counts[...].astype(f32), loads.astype(f32), jnp.zeros((4, SEG - 17), f32)], axis=1
    )
    out[0:8, :] = jnp.concatenate([top, low], axis=0)
    out[8:16, :] = nbr[8:16, :].astype(f32)


def payload_of(load, place, kind, shells, counts, nbr):
    vmem = pl.BlockSpec(memory_space=pltpu.VMEM)
    return pl.pallas_call(
        payload_kernel,
        out_shape=jax.ShapeDtypeStruct((16, SEG), f32),
        in_specs=[pl.BlockSpec(memory_space=pltpu.SMEM)] + [vmem] * 8,
        out_specs=vmem,
        name="payload",
    )(load, place, kind[None], *shells, counts, nbr)


def all_weights(w_embed1, w_embed2, w_v0, w_env, w_lat1, w_lat2, w_gate, w_mix, w_out1, w_out2):
    return (
        w_embed1.T, w_embed2, w_v0, w_env, jnp.swapaxes(w_lat1, 1, 2), w_lat2, w_gate, w_mix,
        w_out1, w_out2[None],
    )


def beside(cells, axis, step):
    count = lax.axis_size(axis)
    return lax.ppermute(cells, axis, [(i, (i + step) % count) for i in range(count)])


def helper(cells):
    count = lax.axis_size("dom")
    return lax.ppermute(cells, "dom", [(i, i ^ 8) for i in range(count)])


def local(
    positions,
    species,
    ghost_index,
    bin_load,
    neighbour,
    pair_count,
    species_shift,
    w_embed1,
    w_embed2,
    w_v0,
    w_env,
    w_lat1,
    w_lat2,
    w_gate,
    w_mix,
    w_out1,
    w_out2,
):
    atoms = positions.shape[1]
    bins, pairs = neighbour.shape
    centers = pair_count.shape[1]
    ghosts = ghost_index.shape[0]
    load = bin_load[0]
    named = ghost_index[:, None] == jnp.arange(atoms)[None, :]
    counts = pair_count.T
    shell = shell_of(ghost_index, positions, species)
    received = [beside(shell, "grp", 1), beside(shell, "grp", -1), beside(shell, "dom", 1), beside(shell, "dom", -1)]
    weights = all_weights(
        w_embed1, w_embed2, w_v0, w_env, w_lat1, w_lat2, w_gate, w_mix, w_out1, w_out2
    )
    mine = payload_of(bin_load, positions, species, received, counts, neighbour)
    other = helper(mine)
    other_counts = other[4:8, 0:bins].astype(jnp.int32)
    other_load = other[4, bins : bins + 1].astype(jnp.int32)
    both = run_forces(bin_load, counts, other_load, other_counts, mine, other, neighbour, weights)
    result = both[0] + helper(both[1])
    energies = result[3, :atoms]
    force = result[0:3, :atoms]
    ghost = result[0:3, atoms : atoms + 4 * ghosts].reshape(3, 4, ghosts)
    back = (
        beside(ghost[:, 0], "grp", -1)
        + beside(ghost[:, 1], "grp", 1)
        + beside(ghost[:, 2], "dom", -1)
        + beside(ghost[:, 3], "dom", 1)
    )
    forces = force + jnp.sum(jnp.where(named[None], back[:, :, None], 0.0), axis=1)
    live = jnp.arange(atoms) // centers < load
    kind_range = jnp.arange(species_shift.shape[0])
    shift = jnp.sum(
        jnp.where(species[:, None] == kind_range[None], species_shift[None, :], 0.0), axis=1
    )
    return (forces, energies + jnp.where(live, shift, 0.0))


def solution(mesh):
    spread_over = ("grp", "dom")
    in_specs = (
        P(None, spread_over),
        P(spread_over),
        P(spread_over),
        P(spread_over),
        P(spread_over, None),
        P(spread_over, None),
    ) + (P(),) * 11
    out_specs = (P(None, spread_over), P(spread_over))
    return jax.shard_map(local, mesh=mesh, in_specs=in_specs, out_specs=out_specs, check_vma=False)
```

```python
import functools
import math

import jax
import jax.numpy as jnp
from jax import lax
from jax.experimental import pallas as pl
from jax.experimental.pallas import tpu as pltpu
from jax.sharding import PartitionSpec as P

f32 = jnp.float32
bf16 = jnp.bfloat16
highest = lax.Precision.HIGHEST
SEG = 256
BIN_ROWS = 16
FORCES_MIB = 60
SLOTS = 8
LANES = 128
CH = 64
ROOT3 = math.sqrt(3.0)
ROOT5 = math.sqrt(5.0)
ROOT15 = math.sqrt(15.0)
HALF = math.sqrt(0.5)
ORDER = (0, 1, 1, 1, 2, 2, 2, 2, 2)
Y_V, Y_W0, Y_Z2, Y_Q = 0, 64, 128, 384
Q_W1, Q_GATE, Q_Z3, Q_OUT = 0, 64, 128, 384
D_W1, D_GATE, D_Z3, D_OUT, D_Z2, D_V, D_W0 = 0, 192, 384, 1152, 1536, 2304, 2496
D_ALL = 2688


def dot(left, right):
    return lax.dot_general(left, right, (((1,), (0,)), ((), ())), preferred_element_type=f32)


def dot_nt(left, right):
    return lax.dot_general(left, right, (((1,), (1,)), ((), ())), preferred_element_type=f32)


def split(value):
    high = value.astype(bf16)
    return high, (value - high.astype(f32)).astype(bf16)


def put3(ref, base, count, row, lanes, value):
    high, low = split(value)
    rows = value.shape[0]
    ref[pl.ds(base + row, rows), lanes] = high
    ref[pl.ds(base + count + row, rows), lanes] = high
    ref[pl.ds(base + 2 * count + row, rows), lanes] = low


def put2(high_ref, low_ref, row, lanes, value):
    high, low = split(value)
    rows = value.shape[0]
    high_ref[pl.ds(row, rows), lanes] = high
    low_ref[pl.ds(row, rows), lanes] = low


RAW_SHAPES = (
    (24, 256), (256, 256), (64, 256), (2, 64, 256), (2, 448, 256), (2, 256, 256), (1, 64, 256),
    (1, 3, 64, 64), (128, 256), (1, 128),
)
READY_SHAPES = (
    (896, 768), (512, 768), (256, 576), (256, 576), (128, 768), (3, 64, 192),
    (256, D_ALL), (256, 1536), (192, 768), (192, 768), (256, 384), (3, 64, 192),
    (256, 64), (16, 768),
)


def prepare_weights(raw, ready, full, tall):
    emb1, emb2, v0, env, lat1, lat2, gate, mix, out1, out2 = raw
    ca, c0, lb0, lb1, c1, mx, cat, c0t, lb0t, lb1t, c1t, mxt, w1, e1t, wide = ready

    def mul(left, right):
        return jnp.dot(left, right, precision=highest, preferred_element_type=f32)

    def triple(value):
        high, low = split(value)
        return jnp.concatenate([high, low, high], axis=1)

    def triple_t(target, column, value):
        high = value.astype(bf16).astype(f32)
        low = (value - high).astype(bf16).astype(f32)
        rows = value.shape[0]
        tall[pl.ds(column, rows), :] = high
        tall[pl.ds(column + rows, rows), :] = low
        tall[pl.ds(column + 2 * rows, rows), :] = high

    def turn(target, rows):
        for at in range(0, rows, LANES):
            target[:, at : at + LANES] = jnp.transpose(tall[at : at + LANES, :]).astype(bf16)

    kinds_h, kinds_l = (x.astype(f32) for x in split(emb1[0:16]))
    basis_h, basis_l = (x.astype(f32) for x in split(emb1[16:24]))
    tall[0:LANES] = jnp.concatenate(
        [kinds_h, kinds_l, basis_h, basis_h, basis_l, basis_l, jnp.zeros((64, 256), f32)], axis=0
    )
    w1[...] = jnp.transpose(tall[0:LANES]).astype(bf16)[:, 0:64]
    e1t[...] = jnp.concatenate(
        [jnp.concatenate([basis_h, basis_l, basis_h], axis=1), jnp.zeros((8, 768), f32)], axis=0
    ).astype(bf16)
    wide[...] = jnp.transpose(jnp.broadcast_to(out2[...], (LANES, LANES)))
    lat1_a = [jnp.transpose(lat1[layer, 0:256]) for layer in range(2)]
    late = jnp.concatenate(
        [env[1] * (0.125 * HALF), gate[0] * HALF, lat1_a[1] * HALF, out1[...] * (HALF * HALF)],
        axis=0,
    )
    early = jnp.concatenate([v0[...], env[0] * 0.125, lat1_a[0]], axis=0)
    full[0:384] = mul(early, emb2[...])
    full[384:896] = mul(late, emb2[...])
    ca[...] = triple(full[...])
    for column, start, rows in (
        (D_W1, 384, 64), (D_GATE, 448, 64), (D_Z3, 512, 256), (D_OUT, 768, 128),
        (D_Z2, 128, 256), (D_V, 0, 64), (D_W0, 64, 64),
    ):
        triple_t(cat, column, full[start : start + rows])
    turn(cat, D_ALL)
    full[0:512] = mul(late, lat2[0])
    c0[...] = triple(full[0:512])
    for column, start, rows in ((D_W1, 0, 64), (D_GATE, 64, 64), (D_Z3, 128, 256), (D_OUT, 384, 128)):
        triple_t(c0t, column, full[start : start + rows])
    turn(c0t, 1536)
    full[0:128] = mul(out1[...] * HALF, lat2[1])
    c1[...] = triple(full[0:128])
    triple_t(c1t, 0, full[0:128])
    turn(c1t, 384)
    for layer, ahead, back in ((0, lb0, lb0t), (1, lb1, lb1t)):
        part = lat1[layer, 256:448]
        ahead[...] = triple(jnp.transpose(part))
        back[...] = triple(part)
    for order in range(3):
        mx[order] = triple(mix[0, order])
        mxt[order] = triple(jnp.transpose(mix[0, order]))


def scratch_list(width):
    w, s = width, width // SEG
    return dict(
        oh=((384, w), bf16), sb=((256, w), bf16), sf=((SLOTS, w), f32), hb=((256, w), bf16),
        x1=((64, w), bf16), a=((768, w), bf16), s0=((576, w), bf16), dy=((D_ALL, w), bf16),
        u=((1728, w), bf16), dg=((576, 2 * w), bf16),
        wh=((320, w), bf16), wl=((320, w), bf16),
        y=((896, w), f32), q=((512, w), f32),
        sa=((256, w), f32), da=((256, w), f32), sbb=((256, w), f32), dbb=((256, w), f32),
        sc=((256, w), f32), dc=((256, w), f32),
        a0=((192, w), f32), g0=((576, w), f32), g1=((576, w), f32), bm=((576, w), f32),
        t=((576, w), f32), vg=((64, w), f32), dv=((64, w), f32),
        gm=((2 * s, 64, LANES), f32), gd=((2 * s, 64, LANES), f32),
    )


NAMES = tuple(scratch_list(512))


class Stream:
    def __init__(self, refs, width, held):
        for name, ref in zip(NAMES, refs):
            if width < held and name not in ("gm", "gd"):
                ref = ref.at[:, 0 : 2 * width if name == "dg" else width]
            setattr(self, name, ref)
        self.b = self.c = self.a
        self.s1, self.dt, self.du = self.s0, self.u, self.g1
        self.width = width
        self.segs = [slice(i * SEG, (i + 1) * SEG) for i in range(width // SEG)]
        self.all = slice(0, width)


def order_mask(order):
    lane = lax.broadcasted_iota(jnp.int32, (64, LANES), 1)
    low, high = ((0, 8), (8, 32), (32, 72))[order]
    return (lane >= low) & (lane < high)


def sublane_sum(value):
    return jnp.sum(value, axis=0, keepdims=True)


def fold(value):
    rows, lanes = value.shape
    return jnp.sum(value.reshape(rows // 8, 8, lanes), axis=0)


def deal(own_end, other_start, other_end, mine, other, table, deals, sem):
    row = lax.broadcasted_iota(jnp.int32, (LANES, 1), 0)
    center = (row & 15) * 4 + (lax.shift_right_logical(row, 4) & 3)
    low_end = jnp.where(row < 64, 0, other_start)
    high_end = jnp.where(row < 64, own_end, other_end)
    live = (center >= low_end) & (center < high_end)
    parts = []
    for source in (mine, other):
        turned = jnp.transpose(
            jnp.concatenate([source[0:8, 0:LANES], jnp.zeros((120, LANES), f32)], axis=0)
        )
        parts = parts + [turned[0:16, 4 + p : 5 + p] for p in range(4)]
    pairs = jnp.where(live, jnp.concatenate(parts, axis=0), 0.0)
    place = row.astype(f32)
    key = jnp.where(live, pairs * 256.0 + (255.0 - place), -1.0 - place)
    key = jnp.broadcast_to(key, (LANES, LANES))
    rank = jnp.sum((jnp.transpose(key) > key).astype(f32), axis=1, keepdims=True)
    lane = lax.broadcasted_iota(jnp.int32, (LANES, LANES), 1).astype(f32)
    count = own_end + other_end - other_start

    def dealt(segments):
        many = segments.astype(f32)
        turn = jnp.floor((rank + 0.5) / many)
        spot = rank - turn * many
        odd = turn - 2.0 * jnp.floor(0.5 * turn)
        return turn, jnp.where(odd > 0.5, many - 1.0 - spot, spot)

    def too_full(segments):
        _, seat = dealt(segments)
        load = jnp.sum(jnp.where(lane == seat, pairs, 0.0), axis=0, keepdims=True)
        return jnp.max(load) > float(SEG)

    total = jnp.sum(pairs).astype(jnp.int32)
    first = jnp.maximum(
        lax.shift_right_logical(total + (SEG - 1), 8), lax.shift_right_logical(count + 7, 3)
    )
    segments = lax.while_loop(too_full, lambda s: s + 1, jnp.maximum(first, 1))
    turn, seat = dealt(segments)
    hit = (lane == seat * SLOTS + turn) & live
    names = jnp.sum(jnp.where(hit, place + 1.0, 0.0), axis=0, keepdims=True)
    sizes = jnp.sum(jnp.where(hit, pairs, 0.0), axis=0, keepdims=True)
    table[...] = jnp.concatenate([names, sizes, jnp.zeros((6, LANES), f32)], axis=0).astype(jnp.int32)
    copy = pltpu.make_async_copy(table, deals, sem)
    copy.start()
    copy.wait()
    return segments


def pack(deals, tab, names_ref, lanes, st, seg):
    lane = lax.broadcasted_iota(jnp.int32, (1, SEG), 1)
    slot_row = lax.broadcasted_iota(jnp.int32, (SLOTS, SEG), 0)
    slot_lane = lax.broadcasted_iota(jnp.int32, (SLOTS, SEG), 1)
    inside = jnp.zeros((SLOTS, SEG), jnp.bool_)
    names = jnp.full((1, SEG), -1, jnp.int32)
    mine = jnp.full((1, SEG), -1, jnp.int32)
    filled = jnp.int32(0)
    for j in range(SLOTS):
        at = jnp.maximum(deals[0, seg * SLOTS + j] - 1, 0)
        count = deals[1, seg * SLOTS + j]
        owner = lax.shift_right_logical(at, 6)
        part, bin_at = lax.shift_right_logical(at, 4) & 3, at & 15
        row = names_ref[pl.ds(owner * BIN_ROWS + bin_at, 1), :] + owner * LANES
        row = pltpu.roll(row, (filled + SEG - 64 * part) & (SEG - 1), axis=1)
        here = (lane >= filled) & (lane < filled + count)
        names = jnp.where(here, row, names)
        mine = jnp.where(here, owner * 64 + bin_at * 4 + part, mine)
        inside = inside | (
            (slot_row == j) & (slot_lane >= filled) & (slot_lane < filled + count)
        )
        filled = filled + count
    seats = inside.astype(f32)
    st.sf[:, lanes] = seats
    both = jnp.concatenate([seats, jnp.zeros_like(seats)], axis=0).astype(bf16)
    st.sb[0:16, lanes] = both
    st.sb[128:144, lanes] = both
    for row in range(0, 256, 32):
        atom = lax.broadcasted_iota(jnp.int32, (32, SEG), 0) + row
        st.oh[row : row + 32, lanes] = (atom == names).astype(f32).astype(bf16)
    for row in range(0, LANES, 32):
        atom = lax.broadcasted_iota(jnp.int32, (32, SEG), 0) + row
        st.oh[256 + row : 256 + row + 32, lanes] = (atom == mine).astype(f32).astype(bf16)
    return dot(tab[...], st.oh[:, lanes])


def spread(seg_gamma, seats):
    parts = [
        seg_gamma if m == 0 else pltpu.roll(seg_gamma, LANES - 8 * m, axis=1) for m in range(9)
    ]
    high, low = split(jnp.concatenate(parts, axis=0))
    return dot(jnp.concatenate([high, low], axis=1), seats)


def gather_gamma(parts):
    total = parts[0:64]
    for m in range(1, 9):
        total = total + pltpu.roll(parts[64 * m : 64 * m + 64], 8 * m, axis=1)
    return total


def with_harmonics(value, hb):
    high, low = split(value)
    return dot(jnp.concatenate([high, high], axis=1), hb) + dot(low, hb[0:LANES])


def over_harmonics(high, low, hb):
    first = dot_nt(high, hb)
    return first[:, :LANES] + first[:, LANES:] + dot_nt(low, hb[0:LANES])


def gate_curve(value):
    sig = 0.5 * jnp.tanh(0.5 * value) + 0.5
    act = value * sig
    return act, sig + act * (1.0 - sig)


def activate(st, product, base_ref, base_row, act_ref, slope_ref, target, env):
    for lanes in st.segs:
        scale = env[:, lanes]
        for row in range(0, 256, 32):
            value = product[row : row + 32, lanes]
            if base_ref is not None:
                value = value + base_ref[base_row + row : base_row + row + 32, lanes]
            act, slope = gate_curve(value)
            act_ref[row : row + 32, lanes] = act
            slope_ref[row : row + 32, lanes] = slope * scale
            put3(target, 0, 256, row, lanes, act * scale)


def deactivate(st, product, act_ref, slope_ref, target, base):
    sums = []
    for lanes in st.segs:
        total = jnp.zeros((8, SEG), f32)
        for row in range(0, 256, 32):
            value = product[row : row + 32, lanes]
            total = total + fold(value * act_ref[row : row + 32, lanes])
            put3(target, base, 256, row, lanes, value * slope_ref[row : row + 32, lanes])
        sums.append(sublane_sum(total))
    return jnp.concatenate(sums, axis=1)


def tile(st, w, deals, tab, names_ref, out, first):
    ca, c0, lb0, lb1, c1, mx, cat, c0t, lb0t, lb1t, c1t, mxt, w1, e1t, w2 = w
    got = jnp.concatenate(
        [pack(deals, tab, names_ref, lanes, st, first + i) for i, lanes in enumerate(st.segs)], axis=1
    )
    off = got[0:8] + got[8:16] + got[16:24]
    ox, oy, oz = off[0:1], off[1:2], off[2:3]
    st.x1[0:16, :] = got[24:40].astype(bf16)
    st.x1[16:32, :] = got[24:40].astype(bf16)
    dist_sq = ox * ox + oy * oy + oz * oz + 0.25
    dist = jnp.sqrt(dist_sq)
    inv = 1.0 / dist
    ux, uy, uz = ox * inv, oy * inv, oz * inv
    harm = [
        None, ROOT3 * ux, ROOT3 * uy, ROOT3 * uz, ROOT15 * ux * uy, ROOT15 * uy * uz,
        0.5 * ROOT5 * (2.0 * uz * uz - ux * ux - uy * uy), ROOT15 * ux * uz,
        0.5 * ROOT15 * (ux * ux - uy * uy),
    ]
    ratio = dist_sq * 0.0625
    env = 1.0 / (1.0 + ratio * ratio)
    angle = dist * (math.pi / 8.0)
    sin1, cos1 = jnp.sin(angle), jnp.cos(angle)
    sines, cosines = [sin1], [cos1]
    for _ in range(7):
        s, c = sines[-1], cosines[-1]
        sines.append(s * cos1 + c * sin1)
        cosines.append(c * cos1 - s * sin1)
    sines, cosines = jnp.concatenate(sines, axis=0), jnp.concatenate(cosines, axis=0)
    level = 0.5 * inv * env
    high = (sines * level).astype(bf16).astype(f32)
    pair = jnp.concatenate([high, sines * level - high], axis=0).astype(bf16)
    st.x1[32:48, :] = pair
    st.x1[48:64, :] = pair
    for lanes in st.segs:
        seats = st.sf[:, lanes]
        blocks = [seats] + [harm[m][:, lanes] * seats for m in range(1, 9)] + [jnp.zeros_like(seats)]
        for k in range(0, 10, 2):
            block = jnp.concatenate(blocks[k : k + 2], axis=0)
            h, l = split(block)
            st.hb[8 * k : 8 * k + 16, lanes] = h
            st.hb[LANES + 8 * k : LANES + 8 * k + 16, lanes] = l
    activate(st, dot(w1[...], st.x1[...]), None, 0, st.sa, st.da, st.a, env)
    st.y[...] = dot(ca[...], st.a[...])
    for i, lanes in enumerate(st.segs):
        put2(st.wh, st.wl, 64, lanes, st.y[Y_W0 : Y_W0 + 64, lanes])
        hb = st.hb[:, lanes]
        gamma = over_harmonics(st.wh[64:128, lanes], st.wl[64:128, lanes], hb)
        st.gm[i] = gamma
        masked = jnp.concatenate([jnp.where(order_mask(l), gamma, 0.0) for l in range(3)], axis=0)
        scale = with_harmonics(masked, hb)
        st.a0[:, lanes] = scale
        for row in range(0, 192, 32):
            value = st.y[Y_V + row % 64 : Y_V + row % 64 + 32, lanes]
            put3(st.s0, 0, 192, row, lanes, value * scale[row : row + 32])
    activate(st, dot(lb0[...], st.s0[...]), st.y, Y_Z2, st.sbb, st.dbb, st.b, env)
    st.q[...] = dot(c0[...], st.b[...]) + st.y[Y_Q : Y_Q + 512, :]
    for i, lanes in enumerate(st.segs):
        st.g0[:, lanes] = spread(st.gm[i], st.sb[:, lanes])
        put2(st.wh, st.wl, 0, lanes, st.q[Q_W1 : Q_W1 + 64, lanes])
        hb = st.hb[:, lanes]
        gamma = over_harmonics(st.wh[0:64, lanes], st.wl[0:64, lanes], hb)
        st.gm[len(st.segs) + i] = gamma
        st.g1[:, lanes] = spread(gamma, st.sb[:, lanes])
    for lanes in st.segs:
        h = [None] + [harm[m][:, lanes] for m in range(1, 9)]
        for row in range(0, 64, 16):
            vg = st.y[Y_V + row : Y_V + row + 16, lanes] * st.q[Q_GATE + row : Q_GATE + row + 16, lanes]
            st.vg[row : row + 16, lanes] = vg
            g = [st.g0[64 * m + row : 64 * m + row + 16, lanes] for m in range(9)]
            mixed = [g[0]] + [g[m] + g[0] * h[m] for m in range(1, 9)]
            mixed[1] = mixed[1] + (h[2] * g[3] - h[3] * g[2])
            mixed[2] = mixed[2] + (h[3] * g[1] - h[1] * g[3])
            mixed[3] = mixed[3] + (h[1] * g[2] - h[2] * g[1])
            for m in range(9):
                st.bm[64 * m + row : 64 * m + row + 16, lanes] = mixed[m]
                put3(st.u, 192 * m, 64, row, lanes, vg * mixed[m])
    for m in range(9):
        st.t[64 * m : 64 * m + 64, :] = dot(mx[ORDER[m]], st.u[192 * m : 192 * m + 192, :])
    for lanes in st.segs:
        for row in range(0, 64, 16):
            total = [None, None, None]
            for m in range(9):
                at = slice(64 * m + row, 64 * m + row + 16)
                term = st.t[at, lanes] * st.g1[at, lanes]
                o = ORDER[m]
                total[o] = term if total[o] is None else total[o] + term
            for o in range(3):
                put3(st.s1, 0, 192, 64 * o + row, lanes, total[o])
    activate(st, dot(lb1[...], st.s1[...]), st.q, Q_Z3, st.sc, st.dc, st.c, env)
    final = dot(c1[...], st.c[...])
    valid = sublane_sum(st.sf[...])
    reads = []
    for lanes in st.segs:
        total = jnp.zeros((8, SEG), f32)
        scale = env[:, lanes] * valid[:, lanes]
        for row in range(0, 128, 32):
            value = final[row : row + 32, lanes] + st.q[Q_OUT + row : Q_OUT + row + 32, lanes]
            act, slope = gate_curve(value)
            weight = w2[row : row + 32, :]
            weight = jnp.concatenate([weight, weight], axis=1)
            total = total + fold(act * weight)
            put3(st.dy, D_OUT, 128, row, lanes, slope * weight * scale)
        reads.append(sublane_sum(total))
    read = jnp.concatenate(reads, axis=1) * valid
    energy = read * env
    d_env = deactivate(st, dot(c1t[...], st.dy[D_OUT : D_OUT + 384, :]), st.sc, st.dc, st.dy, D_Z3)
    d_scal = dot(lb1t[...], st.dy[D_Z3 : D_Z3 + 768, :])
    for i, lanes in enumerate(st.segs):
        for row in range(0, 64, 16):
            for m in range(9):
                at = slice(64 * m + row, 64 * m + row + 16)
                part = d_scal[64 * ORDER[m] + row : 64 * ORDER[m] + row + 16, lanes]
                put3(st.dt, 192 * m, 64, row, lanes, st.g1[at, lanes] * part)
                high, low = split(st.t[at, lanes] * part)
                st.dg[at, 2 * SEG * i : 2 * SEG * i + SEG] = high
                st.dg[at, 2 * SEG * i + SEG : 2 * SEG * i + 2 * SEG] = low
    for i, lanes in enumerate(st.segs):
        seats = st.sb[0:LANES, lanes]
        seats = jnp.concatenate([seats, seats], axis=1)
        d_gamma = gather_gamma(dot_nt(st.dg[:, 2 * SEG * i : 2 * SEG * i + 2 * SEG], seats))
        st.gd[len(st.segs) + i] = d_gamma
        d_weight = with_harmonics(d_gamma, st.hb[:, lanes])
        put3(st.dy, D_W1, 64, 0, lanes, d_weight)
    for m in range(9):
        st.du[64 * m : 64 * m + 64, :] = dot(mxt[ORDER[m]], st.dt[192 * m : 192 * m + 192, :])
    d_harm = []
    for i, lanes in enumerate(st.segs):
        h = [None] + [harm[m][:, lanes] for m in range(1, 9)]
        sums = [jnp.zeros((8, SEG), f32) for _ in range(8)]
        for row in range(0, 64, 16):
            rows = slice(row, row + 16)
            vg = st.vg[rows, lanes]
            d_vg = jnp.zeros((16, SEG), f32)
            d = []
            for m in range(9):
                at = slice(64 * m + row, 64 * m + row + 16)
                grad = st.du[at, lanes]
                d_vg = d_vg + grad * st.bm[at, lanes]
                d.append(grad * vg)
            value = st.y[Y_V + row : Y_V + row + 16, lanes]
            gate = st.q[Q_GATE + row : Q_GATE + row + 16, lanes]
            put3(st.dy, D_GATE, 64, row, lanes, value * d_vg)
            st.dv[rows, lanes] = gate * d_vg
            g = [st.g0[64 * m + row : 64 * m + row + 16, lanes] for m in range(4)]
            terms = [g[0] * d[m] for m in range(1, 9)]
            terms[0] = terms[0] + (g[2] * d[3] - g[3] * d[2])
            terms[1] = terms[1] + (g[3] * d[1] - g[1] * d[3])
            terms[2] = terms[2] + (g[1] * d[2] - g[2] * d[1])
            sums = [a + fold(b) for a, b in zip(sums, terms)]
            first = d[0]
            for m in range(1, 9):
                first = first + h[m] * d[m]
            back = [first] + d[1:]
            back[1] = back[1] + (h[3] * d[2] - h[2] * d[3])
            back[2] = back[2] + (h[1] * d[3] - h[3] * d[1])
            back[3] = back[3] + (h[2] * d[1] - h[1] * d[2])
            for m in range(9):
                at = slice(64 * m + row, 64 * m + row + 16)
                high, low = split(back[m])
                st.dg[at, 2 * SEG * i : 2 * SEG * i + SEG] = high
                st.dg[at, 2 * SEG * i + SEG : 2 * SEG * i + 2 * SEG] = low
        d_harm.append([sublane_sum(x) for x in sums])
    d_env = d_env + deactivate(st, dot(c0t[...], st.dy[0:1536, :]), st.sbb, st.dbb, st.dy, D_Z2)
    d_scal = dot(lb0t[...], st.dy[D_Z2 : D_Z2 + 768, :])
    for i, lanes in enumerate(st.segs):
        for row in range(0, 64, 32):
            rows = slice(row, row + 32)
            value = st.y[Y_V + row : Y_V + row + 32, lanes]
            d_value = st.dv[rows, lanes]
            for o in range(3):
                at = slice(64 * o + row, 64 * o + row + 32)
                part = d_scal[at, lanes]
                d_value = d_value + part * st.a0[at, lanes]
                put2(st.wh, st.wl, 128 + 64 * o + row, lanes, value * part)
            put3(st.dy, D_V, 64, row, lanes, d_value)
        hb = st.hb[:, lanes]
        seats = st.sb[0:LANES, lanes]
        seats = jnp.concatenate([seats, seats], axis=1)
        d_gamma = gather_gamma(dot_nt(st.dg[:, 2 * SEG * i : 2 * SEG * i + 2 * SEG], seats))
        d_scale = over_harmonics(st.wh[128:320, lanes], st.wl[128:320, lanes], hb)
        for o in range(3):
            d_gamma = d_gamma + jnp.where(order_mask(o), d_scale[64 * o : 64 * o + 64], 0.0)
        put3(st.dy, D_W0, 64, 0, lanes, with_harmonics(d_gamma, hb))
        gamma = st.gm[i]
        left = [st.gd[len(st.segs) + i], d_gamma]
        left = left + [jnp.where(order_mask(l), gamma, 0.0) for l in range(3)]
        left = jnp.concatenate([jnp.transpose(x) for x in (
            jnp.concatenate(left[0:2], axis=0), jnp.concatenate(left[2:4], axis=0),
            jnp.concatenate([left[4], jnp.zeros((64, LANES), f32)], axis=0),
        )], axis=1)
        high, low = split(left[0:80])
        high, low = high[:, 0:320], low[:, 0:320]
        d_seated = (
            dot(high, st.wh[:, lanes]) + dot(low, st.wh[:, lanes]) + dot(high, st.wl[:, lanes])
        )
        seats = st.sf[:, lanes]
        for m in range(1, 9):
            d_harm[i][m - 1] = d_harm[i][m - 1] + sublane_sum(d_seated[8 * m : 8 * m + 8] * seats)
    d_env = d_env + deactivate(st, dot(cat[...], st.dy[...]), st.sa, st.da, st.a, 0)
    d_basis = dot(e1t[...], st.a[...])[0:8]
    d_env = d_env + read
    dh = [None] + [jnp.concatenate([x[m] for x in d_harm], axis=1) for m in range(8)]
    dux = ROOT3 * dh[1] + ROOT15 * (uy * dh[4] + uz * dh[7] + ux * dh[8]) - ROOT5 * ux * dh[6]
    duy = ROOT3 * dh[2] + ROOT15 * (ux * dh[4] + uz * dh[5] - uy * dh[8]) - ROOT5 * uy * dh[6]
    duz = ROOT3 * dh[3] + ROOT15 * (uy * dh[5] + ux * dh[7]) + 2.0 * ROOT5 * uz * dh[6]
    order = (lax.broadcasted_iota(jnp.int32, (8, st.width), 0) + 1).astype(f32)
    sine_part = sublane_sum(sines * d_basis)
    cos_part = sublane_sum(order * cosines * d_basis)
    d_env = d_env + 0.5 * inv * sine_part
    d_inv = 0.5 * env * sine_part + ox * dux + oy * duy + oz * duz
    d_dist = (math.pi / 8.0) * level * cos_part
    d_sq = -0.125 * ratio * env * env * d_env + 0.5 * inv * d_dist - 0.5 * inv * inv * inv * d_inv
    d_sq = 2.0 * d_sq
    grad = [inv * dux + d_sq * ox, inv * duy + d_sq * oy, inv * duz + d_sq * oz]
    rows = jnp.concatenate(grad + [energy, jnp.zeros((4, st.width), f32)], axis=0)
    for lanes in st.segs:
        high = rows[:, lanes].astype(bf16).astype(f32)
        low = rows[:, lanes] - high
        sent = dot_nt(jnp.concatenate([high, low], axis=0).astype(bf16), st.oh[:, lanes])
        out[...] = out[...] + (sent[0:8] + sent[8:16])


def force_kernel(width, load, mine, other, nbr, *rest):
    sources, out, tab, names_ref = rest[:10], rest[10], rest[11], rest[12]
    raw, weights, full, tall, sems = rest[13:23], rest[23:38], rest[38], rest[39], rest[40]
    total, table, deals, scratch = rest[41], rest[42], rest[43], rest[44:]
    copies = [
        pltpu.make_async_copy(source, target, sems.at[i])
        for i, (source, target) in enumerate(zip(sources, raw))
    ]
    for copy in copies:
        copy.start()
    wide = Stream(scratch, width, width)
    narrow = Stream(scratch, width // 2, width)
    total[...] = jnp.zeros_like(total)
    wide.sb[...] = jnp.zeros_like(wide.sb)
    wide.hb[...] = jnp.zeros_like(wide.hb)
    names_ref[0:16, :] = nbr[...]
    names_ref[16:24, :] = jnp.zeros((8, SEG), jnp.int32)
    names_ref[24:32, :] = other[8:16, :].astype(jnp.int32)
    other_load = jnp.max(other[4:5, 16:17]).astype(jnp.int32)
    own_all, other_all = load[0] * 4, other_load * 4
    share = jnp.maximum(2 * (load[0] + other_load), 32)
    segments = deal(
        jnp.minimum(own_all, share), jnp.minimum(other_all, share), other_all,
        mine, other, table, deals, sems.at[10],
    )
    kind = lax.broadcasted_iota(jnp.int32, (8, LANES), 0).astype(f32)
    row = lax.broadcasted_iota(jnp.int32, (8, LANES), 0)
    lane = lax.broadcasted_iota(jnp.int32, (8, LANES), 1)
    firsts, seconds = [], []
    for source in (mine, other):
        value = jnp.where(lane < 96, source[0:8, 0:LANES], 0.0)
        place = jnp.where(row < 3, value, 0.0)
        high = place.astype(bf16).astype(f32)
        rest_of = place - high
        mid = rest_of.astype(bf16).astype(f32)
        low = (rest_of - mid).astype(bf16).astype(f32)
        named = (kind == value[3:4]).astype(f32)
        none = jnp.zeros_like(named)
        firsts.append(jnp.concatenate([high, mid, low, none, named, none], axis=0))
        seconds.append(jnp.concatenate([-high, -mid, -low, named, none, none], axis=0)[:, 0:64])
    tab[...] = jnp.concatenate(firsts + [jnp.concatenate(seconds, axis=1)], axis=1).astype(bf16)
    for copy in copies:
        copy.wait()
    prepare_weights(raw, weights, full, tall)
    tiles = lax.shift_right_logical(segments + 1, 2)

    def step(at, carry):
        tile(wide, weights, deals, tab, names_ref, total, at * 4)
        return carry

    lax.fori_loop(0, tiles, step, 0)

    @pl.when(segments > tiles * 4)
    def _():
        tile(narrow, weights, deals, tab, names_ref, total, tiles * 4)

    none = jnp.zeros((8, 64), f32)
    for owner in range(2):
        start = 2 * LANES + 64 * owner
        centers = jnp.concatenate([total[:, start : start + 64], none], axis=1)
        names = total[:, LANES * owner : LANES * owner + LANES]
        out[owner] = jnp.where(row < 3, centers - names, centers)


def run_forces(load, mine, other, nbr, weights, width=1024):
    scratch = scratch_list(width)
    vmem = pl.BlockSpec(memory_space=pltpu.VMEM)
    smem = pl.BlockSpec(memory_space=pltpu.SMEM)
    return pl.pallas_call(
        functools.partial(force_kernel, width),
        out_shape=jax.ShapeDtypeStruct((2, 8, LANES), f32),
        in_specs=[smem] + [vmem] * 3 + [pl.BlockSpec(memory_space=pl.ANY)] * len(weights),
        out_specs=vmem,
        scratch_shapes=[pltpu.VMEM((48, 384), bf16), pltpu.VMEM((32, SEG), jnp.int32)]
        + [pltpu.VMEM(shape, f32) for shape in RAW_SHAPES]
        + [pltpu.VMEM(shape, bf16) for shape in READY_SHAPES]
        + [pltpu.VMEM((128, LANES), f32), pltpu.VMEM((896, 256), f32)]
        + [pltpu.VMEM((D_ALL, 256), f32), pltpu.SemaphoreType.DMA((len(weights) + 1,))]
        + [pltpu.VMEM((8, 384), f32), pltpu.VMEM((8, LANES), jnp.int32)]
        + [pltpu.SMEM((8, LANES), jnp.int32)]
        + [pltpu.VMEM(shape, kind) for shape, kind in scratch.values()],
        compiler_params=pltpu.CompilerParams(vmem_limit_bytes=FORCES_MIB * 2**20),
        name="forces",
    )(load, mine, other, nbr, *weights)


def shell_kernel(ghost, place, kind, out):
    lane = lax.broadcasted_iota(jnp.int32, (8, 64), 1)
    whole = jnp.concatenate([place[...], kind[...].astype(f32), jnp.zeros((4, 64), f32)], axis=0)
    spot = lax.broadcasted_iota(jnp.int32, (8, 8), 1)
    total = jnp.zeros((8, 8), f32)
    for k in range(8):
        one = jnp.sum(jnp.where(lane == ghost[k], whole, 0.0), axis=1, keepdims=True)
        total = total + jnp.where(spot == k, one, 0.0)
    out[...] = total[0:4]


def shell_of(ghost, place, kind):
    vmem = pl.BlockSpec(memory_space=pltpu.VMEM)
    return pl.pallas_call(
        shell_kernel,
        out_shape=jax.ShapeDtypeStruct((4, 8), f32),
        in_specs=[pl.BlockSpec(memory_space=pltpu.SMEM), vmem, vmem],
        out_specs=vmem,
        name="shell",
    )(ghost, place, kind[None])


def payload_kernel(load, place, kind, first, second, third, fourth, counts, nbr, out):
    whole = jnp.concatenate([place[...], kind[...].astype(f32)], axis=0)
    top = jnp.concatenate(
        [whole, first[...], second[...], third[...], fourth[...], jnp.zeros((4, 160), f32)], axis=1
    )
    loads = jnp.zeros((4, 1), jnp.int32) + load[0]
    low = jnp.concatenate(
        [counts[...].astype(f32), loads.astype(f32), jnp.zeros((4, SEG - 17), f32)], axis=1
    )
    out[0:8, :] = jnp.concatenate([top, low], axis=0)
    out[8:16, :] = nbr[8:16, :].astype(f32)


def payload_of(load, place, kind, shells, counts, nbr):
    vmem = pl.BlockSpec(memory_space=pltpu.VMEM)
    return pl.pallas_call(
        payload_kernel,
        out_shape=jax.ShapeDtypeStruct((16, SEG), f32),
        in_specs=[pl.BlockSpec(memory_space=pltpu.SMEM)] + [vmem] * 8,
        out_specs=vmem,
        name="payload",
    )(load, place, kind[None], *shells, counts, nbr)


def all_weights(w_embed1, w_embed2, w_v0, w_env, w_lat1, w_lat2, w_gate, w_mix, w_out1, w_out2):
    return (
        w_embed1.T, w_embed2, w_v0, w_env, jnp.swapaxes(w_lat1, 1, 2), w_lat2, w_gate, w_mix,
        w_out1, w_out2[None],
    )


def beside(cells, axis, step):
    count = lax.axis_size(axis)
    return lax.ppermute(cells, axis, [(i, (i + step) % count) for i in range(count)])


def helper(cells):
    count = lax.axis_size("dom")
    return lax.ppermute(cells, "dom", [(i, i ^ 8) for i in range(count)])


def local(
    positions,
    species,
    ghost_index,
    bin_load,
    neighbour,
    pair_count,
    species_shift,
    w_embed1,
    w_embed2,
    w_v0,
    w_env,
    w_lat1,
    w_lat2,
    w_gate,
    w_mix,
    w_out1,
    w_out2,
):
    atoms = positions.shape[1]
    centers = pair_count.shape[1]
    ghosts = ghost_index.shape[0]
    load = bin_load[0]
    named = ghost_index[:, None] == jnp.arange(atoms)[None, :]
    counts = pair_count.T
    shell = shell_of(ghost_index, positions, species)
    received = [beside(shell, "grp", 1), beside(shell, "grp", -1), beside(shell, "dom", 1), beside(shell, "dom", -1)]
    weights = all_weights(
        w_embed1, w_embed2, w_v0, w_env, w_lat1, w_lat2, w_gate, w_mix, w_out1, w_out2
    )
    mine = payload_of(bin_load, positions, species, received, counts, neighbour)
    other = helper(mine)
    both = run_forces(bin_load, mine, other, neighbour, weights)
    result = both[0] + helper(both[1])
    energies = result[3, :atoms]
    force = result[0:3, :atoms]
    ghost = result[0:3, atoms : atoms + 4 * ghosts].reshape(3, 4, ghosts)
    back = (
        beside(ghost[:, 0], "grp", -1)
        + beside(ghost[:, 1], "grp", 1)
        + beside(ghost[:, 2], "dom", -1)
        + beside(ghost[:, 3], "dom", 1)
    )
    forces = force + jnp.sum(jnp.where(named[None], back[:, :, None], 0.0), axis=1)
    live = jnp.arange(atoms) // centers < load
    kind_range = jnp.arange(species_shift.shape[0])
    shift = jnp.sum(
        jnp.where(species[:, None] == kind_range[None], species_shift[None, :], 0.0), axis=1
    )
    return (forces, energies + jnp.where(live, shift, 0.0))


def solution(mesh):
    spread_over = ("grp", "dom")
    in_specs = (
        P(None, spread_over),
        P(spread_over),
        P(spread_over),
        P(spread_over),
        P(spread_over, None),
        P(spread_over, None),
    ) + (P(),) * 11
    out_specs = (P(None, spread_over), P(spread_over))
    return jax.shard_map(local, mesh=mesh, in_specs=in_specs, out_specs=out_specs, check_vma=False)
```

```python
import functools
import math

import jax
import jax.numpy as jnp
from jax import lax
from jax.experimental import pallas as pl
from jax.experimental.pallas import tpu as pltpu
from jax.sharding import PartitionSpec as P

f32 = jnp.float32
bf16 = jnp.bfloat16
highest = lax.Precision.HIGHEST
SEG = 256
BIN_ROWS = 16
FORCES_MIB = 60
SLOTS = 8
LANES = 128
CH = 64
ROOT3 = math.sqrt(3.0)
ROOT5 = math.sqrt(5.0)
ROOT15 = math.sqrt(15.0)
HALF = math.sqrt(0.5)
ORDER = (0, 1, 1, 1, 2, 2, 2, 2, 2)
Y_V, Y_W0, Y_Z2, Y_Q = 0, 64, 128, 384
Q_W1, Q_GATE, Q_Z3, Q_OUT = 0, 64, 128, 384
D_W1, D_GATE, D_Z3, D_OUT, D_Z2, D_V, D_W0 = 0, 192, 384, 1152, 1536, 2304, 2496
D_ALL = 2688


def dot(left, right):
    return lax.dot_general(left, right, (((1,), (0,)), ((), ())), preferred_element_type=f32)


def dot_nt(left, right):
    return lax.dot_general(left, right, (((1,), (1,)), ((), ())), preferred_element_type=f32)


def split(value):
    high = value.astype(bf16)
    return high, (value - high.astype(f32)).astype(bf16)


def put3(ref, base, count, row, lanes, value):
    high, low = split(value)
    rows = value.shape[0]
    ref[pl.ds(base + row, rows), lanes] = high
    ref[pl.ds(base + count + row, rows), lanes] = high
    ref[pl.ds(base + 2 * count + row, rows), lanes] = low


def put2(high_ref, low_ref, row, lanes, value):
    high, low = split(value)
    rows = value.shape[0]
    high_ref[pl.ds(row, rows), lanes] = high
    low_ref[pl.ds(row, rows), lanes] = low


RAW_SHAPES = (
    (24, 256), (256, 256), (64, 256), (2, 64, 256), (2, 448, 256), (2, 256, 256), (1, 64, 256),
    (1, 3, 64, 64), (128, 256), (1, 128),
)
READY_SHAPES = (
    (896, 768), (512, 768), (256, 576), (256, 576), (128, 768), (3, 64, 192),
    (256, D_ALL), (256, 1536), (192, 768), (192, 768), (256, 384), (3, 64, 192),
    (256, 64), (16, 768),
)


def prepare_weights(raw, ready, full, tall):
    emb1, emb2, v0, env, lat1, lat2, gate, mix, out1, out2 = raw
    ca, c0, lb0, lb1, c1, mx, cat, c0t, lb0t, lb1t, c1t, mxt, w1, e1t, wide = ready

    def mul(left, right):
        return jnp.dot(left, right, precision=highest, preferred_element_type=f32)

    def triple(value):
        high, low = split(value)
        return jnp.concatenate([high, low, high], axis=1)

    def triple_t(target, column, value):
        high = value.astype(bf16).astype(f32)
        low = (value - high).astype(bf16).astype(f32)
        rows = value.shape[0]
        tall[pl.ds(column, rows), :] = high
        tall[pl.ds(column + rows, rows), :] = low
        tall[pl.ds(column + 2 * rows, rows), :] = high

    def turn(target, rows):
        for at in range(0, rows, LANES):
            target[:, at : at + LANES] = jnp.transpose(tall[at : at + LANES, :]).astype(bf16)

    kinds_h, kinds_l = (x.astype(f32) for x in split(emb1[0:16]))
    basis_h, basis_l = (x.astype(f32) for x in split(emb1[16:24]))
    tall[0:LANES] = jnp.concatenate(
        [kinds_h, kinds_l, basis_h, basis_h, basis_l, basis_l, jnp.zeros((64, 256), f32)], axis=0
    )
    w1[...] = jnp.transpose(tall[0:LANES]).astype(bf16)[:, 0:64]
    e1t[...] = jnp.concatenate(
        [jnp.concatenate([basis_h, basis_l, basis_h], axis=1), jnp.zeros((8, 768), f32)], axis=0
    ).astype(bf16)
    wide[...] = jnp.transpose(jnp.broadcast_to(out2[...], (LANES, LANES)))
    lat1_a = [jnp.transpose(lat1[layer, 0:256]) for layer in range(2)]
    late = jnp.concatenate(
        [env[1] * (0.125 * HALF), gate[0] * HALF, lat1_a[1] * HALF, out1[...] * (HALF * HALF)],
        axis=0,
    )
    early = jnp.concatenate([v0[...], env[0] * 0.125, lat1_a[0]], axis=0)
    full[0:384] = mul(early, emb2[...])
    full[384:896] = mul(late, emb2[...])
    ca[...] = triple(full[...])
    for column, start, rows in (
        (D_W1, 384, 64), (D_GATE, 448, 64), (D_Z3, 512, 256), (D_OUT, 768, 128),
        (D_Z2, 128, 256), (D_V, 0, 64), (D_W0, 64, 64),
    ):
        triple_t(cat, column, full[start : start + rows])
    turn(cat, D_ALL)
    full[0:512] = mul(late, lat2[0])
    c0[...] = triple(full[0:512])
    for column, start, rows in ((D_W1, 0, 64), (D_GATE, 64, 64), (D_Z3, 128, 256), (D_OUT, 384, 128)):
        triple_t(c0t, column, full[start : start + rows])
    turn(c0t, 1536)
    full[0:128] = mul(out1[...] * HALF, lat2[1])
    c1[...] = triple(full[0:128])
    triple_t(c1t, 0, full[0:128])
    turn(c1t, 384)
    for layer, ahead, back in ((0, lb0, lb0t), (1, lb1, lb1t)):
        part = lat1[layer, 256:448]
        ahead[...] = triple(jnp.transpose(part))
        back[...] = triple(part)
    for order in range(3):
        mx[order] = triple(mix[0, order])
        mxt[order] = triple(jnp.transpose(mix[0, order]))


def scratch_list(width):
    w, s = width, width // SEG
    return dict(
        oh=((384, w), bf16), sb=((256, w), bf16), sf=((SLOTS, w), f32), hb=((256, w), bf16),
        x1=((64, w), bf16), a=((768, w), bf16), s0=((576, w), bf16), dy=((D_ALL, w), bf16),
        u=((1728, w), bf16), dg=((576, 2 * w), bf16),
        wh=((320, w), bf16), wl=((320, w), bf16),
        y=((896, w), f32), q=((512, w), f32),
        sa=((256, w), f32), da=((256, w), f32), sbb=((256, w), f32), dbb=((256, w), f32),
        sc=((256, w), f32), dc=((256, w), f32),
        a0=((192, w), f32), g0=((576, w), f32), g1=((576, w), f32), bm=((576, w), f32),
        t=((576, w), f32), vg=((64, w), f32), dv=((64, w), f32),
        gm=((2 * s, 64, LANES), f32), gd=((2 * s, 64, LANES), f32),
    )


NAMES = tuple(scratch_list(512))


class Stream:
    def __init__(self, refs, width, held):
        for name, ref in zip(NAMES, refs):
            if width < held and name not in ("gm", "gd"):
                ref = ref.at[:, 0 : 2 * width if name == "dg" else width]
            setattr(self, name, ref)
        self.b = self.c = self.a
        self.s1, self.dt, self.du = self.s0, self.u, self.g1
        self.width = width
        self.segs = [slice(i * SEG, (i + 1) * SEG) for i in range(width // SEG)]
        self.all = slice(0, width)


def order_mask(order):
    lane = lax.broadcasted_iota(jnp.int32, (64, LANES), 1)
    low, high = ((0, 8), (8, 32), (32, 72))[order]
    return (lane >= low) & (lane < high)


def sublane_sum(value):
    return jnp.sum(value, axis=0, keepdims=True)


def fold(value):
    rows, lanes = value.shape
    return jnp.sum(value.reshape(rows // 8, 8, lanes), axis=0)


def deal(own_load, other_load, mine, other, table, deals, sem):
    row = lax.broadcasted_iota(jnp.int32, (LANES, 1), 0)
    center = (row & 15) * 4 + (lax.shift_right_logical(row, 4) & 3)
    parts = []
    for source in (mine, other):
        turned = jnp.transpose(
            jnp.concatenate([source[0:8, 0:LANES], jnp.zeros((120, LANES), f32)], axis=0)
        )
        parts = parts + [turned[0:16, 4 + p : 5 + p] for p in range(4)]
    own_all, other_all = own_load * 4, other_load * 4
    pairs = jnp.where(
        center < jnp.where(row < 64, own_all, other_all), jnp.concatenate(parts, axis=0), 0.0
    )
    place = row.astype(f32)
    spread_out = jnp.broadcast_to(pairs, (LANES, LANES))
    order = jnp.broadcast_to(center.astype(f32), (LANES, LANES))
    side = jnp.where(row < 64, 0.0, 64.0)
    ahead = (jnp.transpose(order) <= order) & (jnp.transpose(side + jnp.zeros_like(order)) == side)
    upto = jnp.sum(jnp.where(ahead, jnp.transpose(spread_out), 0.0), axis=1, keepdims=True)
    kept = (upto <= 0.5 * jnp.sum(pairs) + 24.0) & (pairs > 0.0)
    share = 2 * (own_load + other_load)
    slack = jnp.where(own_load + other_load <= 30, 3, 0)
    low_end, high_end = jnp.maximum(share - slack, 32), jnp.maximum(share + slack, 32)

    def keep(first, count):
        found = jnp.sum(kept[first : first + 64].astype(f32)).astype(jnp.int32)
        return jnp.minimum(jnp.minimum(jnp.maximum(found, low_end), high_end), count)

    own_end, other_start, other_end = keep(0, own_all), keep(64, other_all), other_all
    live = (center >= jnp.where(row < 64, 0, other_start)) & (
        center < jnp.where(row < 64, own_end, other_end)
    )
    pairs = jnp.where(live, pairs, 0.0)
    key = jnp.where(live, pairs * 256.0 + (255.0 - place), -1.0 - place)
    key = jnp.broadcast_to(key, (LANES, LANES))
    rank = jnp.sum((jnp.transpose(key) > key).astype(f32), axis=1, keepdims=True)
    lane = lax.broadcasted_iota(jnp.int32, (LANES, LANES), 1).astype(f32)
    count = own_end + other_end - other_start

    def dealt(segments, turned_last):
        many = segments.astype(f32)
        turn = jnp.floor((rank + 0.5) / many)
        spot = rank - turn * many
        odd = turn - 2.0 * jnp.floor(0.5 * turn)
        final = jnp.floor((count.astype(f32) - 0.5) / many)
        odd = jnp.where(turn == final, jnp.abs(odd - turned_last), odd)
        return turn, jnp.where(odd > 0.5, many - 1.0 - spot, spot)

    def fullest(segments, turned_last):
        _, seat = dealt(segments, turned_last)
        return jnp.max(jnp.sum(jnp.where(lane == seat, pairs, 0.0), axis=0, keepdims=True))

    def too_full(segments):
        return jnp.minimum(fullest(segments, 0.0), fullest(segments, 1.0)) > float(SEG)

    total = jnp.sum(pairs).astype(jnp.int32)
    first = jnp.maximum(
        lax.shift_right_logical(total + (SEG - 1), 8), lax.shift_right_logical(count + 7, 3)
    )
    segments = lax.while_loop(too_full, lambda s: s + 1, jnp.maximum(first, 1))
    turn, seat = dealt(segments, (fullest(segments, 0.0) > float(SEG)).astype(f32))
    hit = (lane == seat * SLOTS + turn) & live
    names = jnp.sum(jnp.where(hit, place + 1.0, 0.0), axis=0, keepdims=True)
    sizes = jnp.sum(jnp.where(hit, pairs, 0.0), axis=0, keepdims=True)
    table[...] = jnp.concatenate([names, sizes, jnp.zeros((6, LANES), f32)], axis=0).astype(jnp.int32)
    copy = pltpu.make_async_copy(table, deals, sem)
    copy.start()
    copy.wait()
    return segments


def pack(deals, tab, names_ref, lanes, st, seg):
    lane = lax.broadcasted_iota(jnp.int32, (1, SEG), 1)
    slot_row = lax.broadcasted_iota(jnp.int32, (SLOTS, SEG), 0)
    slot_lane = lax.broadcasted_iota(jnp.int32, (SLOTS, SEG), 1)
    inside = jnp.zeros((SLOTS, SEG), jnp.bool_)
    names = jnp.full((1, SEG), -1, jnp.int32)
    mine = jnp.full((1, SEG), -1, jnp.int32)
    filled = jnp.int32(0)
    for j in range(SLOTS):
        at = jnp.maximum(deals[0, seg * SLOTS + j] - 1, 0)
        count = deals[1, seg * SLOTS + j]
        owner = lax.shift_right_logical(at, 6)
        part, bin_at = lax.shift_right_logical(at, 4) & 3, at & 15
        row = names_ref[pl.ds(owner * BIN_ROWS + bin_at, 1), :] + owner * LANES
        row = pltpu.roll(row, (filled + SEG - 64 * part) & (SEG - 1), axis=1)
        here = (lane >= filled) & (lane < filled + count)
        names = jnp.where(here, row, names)
        mine = jnp.where(here, owner * 64 + bin_at * 4 + part, mine)
        inside = inside | (
            (slot_row == j) & (slot_lane >= filled) & (slot_lane < filled + count)
        )
        filled = filled + count
    seats = inside.astype(f32)
    st.sf[:, lanes] = seats
    both = jnp.concatenate([seats, jnp.zeros_like(seats)], axis=0).astype(bf16)
    st.sb[0:16, lanes] = both
    st.sb[128:144, lanes] = both
    for row in range(0, 256, 32):
        atom = lax.broadcasted_iota(jnp.int32, (32, SEG), 0) + row
        st.oh[row : row + 32, lanes] = (atom == names).astype(f32).astype(bf16)
    for row in range(0, LANES, 32):
        atom = lax.broadcasted_iota(jnp.int32, (32, SEG), 0) + row
        st.oh[256 + row : 256 + row + 32, lanes] = (atom == mine).astype(f32).astype(bf16)
    return dot(tab[...], st.oh[:, lanes])


def spread(seg_gamma, seats):
    parts = [
        seg_gamma if m == 0 else pltpu.roll(seg_gamma, LANES - 8 * m, axis=1) for m in range(9)
    ]
    high, low = split(jnp.concatenate(parts, axis=0))
    return dot(jnp.concatenate([high, low], axis=1), seats)


def gather_gamma(parts):
    total = parts[0:64]
    for m in range(1, 9):
        total = total + pltpu.roll(parts[64 * m : 64 * m + 64], 8 * m, axis=1)
    return total


def with_harmonics(value, hb):
    high, low = split(value)
    return dot(jnp.concatenate([high, high], axis=1), hb) + dot(low, hb[0:LANES])


def over_harmonics(high, low, hb):
    first = dot_nt(high, hb)
    return first[:, :LANES] + first[:, LANES:] + dot_nt(low, hb[0:LANES])


def gate_curve(value):
    sig = 0.5 * jnp.tanh(0.5 * value) + 0.5
    act = value * sig
    return act, sig + act * (1.0 - sig)


def activate(st, product, base_ref, base_row, act_ref, slope_ref, target, env):
    for lanes in st.segs:
        scale = env[:, lanes]
        for row in range(0, 256, 32):
            value = product[row : row + 32, lanes]
            if base_ref is not None:
                value = value + base_ref[base_row + row : base_row + row + 32, lanes]
            act, slope = gate_curve(value)
            act_ref[row : row + 32, lanes] = act
            slope_ref[row : row + 32, lanes] = slope * scale
            put3(target, 0, 256, row, lanes, act * scale)


def deactivate(st, product, act_ref, slope_ref, target, base):
    sums = []
    for lanes in st.segs:
        total = jnp.zeros((8, SEG), f32)
        for row in range(0, 256, 32):
            value = product[row : row + 32, lanes]
            total = total + fold(value * act_ref[row : row + 32, lanes])
            put3(target, base, 256, row, lanes, value * slope_ref[row : row + 32, lanes])
        sums.append(sublane_sum(total))
    return jnp.concatenate(sums, axis=1)


def tile(st, w, deals, tab, names_ref, out, first):
    ca, c0, lb0, lb1, c1, mx, cat, c0t, lb0t, lb1t, c1t, mxt, w1, e1t, w2 = w
    got = jnp.concatenate(
        [pack(deals, tab, names_ref, lanes, st, first + i) for i, lanes in enumerate(st.segs)], axis=1
    )
    off = got[0:8] + got[8:16] + got[16:24]
    ox, oy, oz = off[0:1], off[1:2], off[2:3]
    st.x1[0:16, :] = got[24:40].astype(bf16)
    st.x1[16:32, :] = got[24:40].astype(bf16)
    dist_sq = ox * ox + oy * oy + oz * oz + 0.25
    dist = jnp.sqrt(dist_sq)
    inv = 1.0 / dist
    ux, uy, uz = ox * inv, oy * inv, oz * inv
    harm = [
        None, ROOT3 * ux, ROOT3 * uy, ROOT3 * uz, ROOT15 * ux * uy, ROOT15 * uy * uz,
        0.5 * ROOT5 * (2.0 * uz * uz - ux * ux - uy * uy), ROOT15 * ux * uz,
        0.5 * ROOT15 * (ux * ux - uy * uy),
    ]
    ratio = dist_sq * 0.0625
    env = 1.0 / (1.0 + ratio * ratio)
    angle = dist * (math.pi / 8.0)
    sin1, cos1 = jnp.sin(angle), jnp.cos(angle)
    sines, cosines = [sin1], [cos1]
    for _ in range(7):
        s, c = sines[-1], cosines[-1]
        sines.append(s * cos1 + c * sin1)
        cosines.append(c * cos1 - s * sin1)
    sines, cosines = jnp.concatenate(sines, axis=0), jnp.concatenate(cosines, axis=0)
    level = 0.5 * inv * env
    high = (sines * level).astype(bf16).astype(f32)
    pair = jnp.concatenate([high, sines * level - high], axis=0).astype(bf16)
    st.x1[32:48, :] = pair
    st.x1[48:64, :] = pair
    for lanes in st.segs:
        seats = st.sf[:, lanes]
        blocks = [seats] + [harm[m][:, lanes] * seats for m in range(1, 9)] + [jnp.zeros_like(seats)]
        for k in range(0, 10, 2):
            block = jnp.concatenate(blocks[k : k + 2], axis=0)
            h, l = split(block)
            st.hb[8 * k : 8 * k + 16, lanes] = h
            st.hb[LANES + 8 * k : LANES + 8 * k + 16, lanes] = l
    activate(st, dot(w1[...], st.x1[...]), None, 0, st.sa, st.da, st.a, env)
    st.y[...] = dot(ca[...], st.a[...])
    for i, lanes in enumerate(st.segs):
        put2(st.wh, st.wl, 64, lanes, st.y[Y_W0 : Y_W0 + 64, lanes])
        hb = st.hb[:, lanes]
        gamma = over_harmonics(st.wh[64:128, lanes], st.wl[64:128, lanes], hb)
        st.gm[i] = gamma
        masked = jnp.concatenate([jnp.where(order_mask(l), gamma, 0.0) for l in range(3)], axis=0)
        scale = with_harmonics(masked, hb)
        st.a0[:, lanes] = scale
        for row in range(0, 192, 32):
            value = st.y[Y_V + row % 64 : Y_V + row % 64 + 32, lanes]
            put3(st.s0, 0, 192, row, lanes, value * scale[row : row + 32])
    activate(st, dot(lb0[...], st.s0[...]), st.y, Y_Z2, st.sbb, st.dbb, st.b, env)
    st.q[...] = dot(c0[...], st.b[...]) + st.y[Y_Q : Y_Q + 512, :]
    for i, lanes in enumerate(st.segs):
        st.g0[:, lanes] = spread(st.gm[i], st.sb[:, lanes])
        put2(st.wh, st.wl, 0, lanes, st.q[Q_W1 : Q_W1 + 64, lanes])
        hb = st.hb[:, lanes]
        gamma = over_harmonics(st.wh[0:64, lanes], st.wl[0:64, lanes], hb)
        st.gm[len(st.segs) + i] = gamma
        st.g1[:, lanes] = spread(gamma, st.sb[:, lanes])
    for lanes in st.segs:
        h = [None] + [harm[m][:, lanes] for m in range(1, 9)]
        for row in range(0, 64, 16):
            vg = st.y[Y_V + row : Y_V + row + 16, lanes] * st.q[Q_GATE + row : Q_GATE + row + 16, lanes]
            st.vg[row : row + 16, lanes] = vg
            g = [st.g0[64 * m + row : 64 * m + row + 16, lanes] for m in range(9)]
            mixed = [g[0]] + [g[m] + g[0] * h[m] for m in range(1, 9)]
            mixed[1] = mixed[1] + (h[2] * g[3] - h[3] * g[2])
            mixed[2] = mixed[2] + (h[3] * g[1] - h[1] * g[3])
            mixed[3] = mixed[3] + (h[1] * g[2] - h[2] * g[1])
            for m in range(9):
                st.bm[64 * m + row : 64 * m + row + 16, lanes] = mixed[m]
                put3(st.u, 192 * m, 64, row, lanes, vg * mixed[m])
    for m in range(9):
        st.t[64 * m : 64 * m + 64, :] = dot(mx[ORDER[m]], st.u[192 * m : 192 * m + 192, :])
    for lanes in st.segs:
        for row in range(0, 64, 16):
            total = [None, None, None]
            for m in range(9):
                at = slice(64 * m + row, 64 * m + row + 16)
                term = st.t[at, lanes] * st.g1[at, lanes]
                o = ORDER[m]
                total[o] = term if total[o] is None else total[o] + term
            for o in range(3):
                put3(st.s1, 0, 192, 64 * o + row, lanes, total[o])
    activate(st, dot(lb1[...], st.s1[...]), st.q, Q_Z3, st.sc, st.dc, st.c, env)
    final = dot(c1[...], st.c[...])
    valid = sublane_sum(st.sf[...])
    reads = []
    for lanes in st.segs:
        total = jnp.zeros((8, SEG), f32)
        scale = env[:, lanes] * valid[:, lanes]
        for row in range(0, 128, 32):
            value = final[row : row + 32, lanes] + st.q[Q_OUT + row : Q_OUT + row + 32, lanes]
            act, slope = gate_curve(value)
            weight = w2[row : row + 32, :]
            weight = jnp.concatenate([weight, weight], axis=1)
            total = total + fold(act * weight)
            put3(st.dy, D_OUT, 128, row, lanes, slope * weight * scale)
        reads.append(sublane_sum(total))
    read = jnp.concatenate(reads, axis=1) * valid
    energy = read * env
    d_env = deactivate(st, dot(c1t[...], st.dy[D_OUT : D_OUT + 384, :]), st.sc, st.dc, st.dy, D_Z3)
    d_scal = dot(lb1t[...], st.dy[D_Z3 : D_Z3 + 768, :])
    for i, lanes in enumerate(st.segs):
        for row in range(0, 64, 16):
            for m in range(9):
                at = slice(64 * m + row, 64 * m + row + 16)
                part = d_scal[64 * ORDER[m] + row : 64 * ORDER[m] + row + 16, lanes]
                put3(st.dt, 192 * m, 64, row, lanes, st.g1[at, lanes] * part)
                high, low = split(st.t[at, lanes] * part)
                st.dg[at, 2 * SEG * i : 2 * SEG * i + SEG] = high
                st.dg[at, 2 * SEG * i + SEG : 2 * SEG * i + 2 * SEG] = low
    for i, lanes in enumerate(st.segs):
        seats = st.sb[0:LANES, lanes]
        seats = jnp.concatenate([seats, seats], axis=1)
        d_gamma = gather_gamma(dot_nt(st.dg[:, 2 * SEG * i : 2 * SEG * i + 2 * SEG], seats))
        st.gd[len(st.segs) + i] = d_gamma
        d_weight = with_harmonics(d_gamma, st.hb[:, lanes])
        put3(st.dy, D_W1, 64, 0, lanes, d_weight)
    for m in range(9):
        st.du[64 * m : 64 * m + 64, :] = dot(mxt[ORDER[m]], st.dt[192 * m : 192 * m + 192, :])
    d_harm = []
    for i, lanes in enumerate(st.segs):
        h = [None] + [harm[m][:, lanes] for m in range(1, 9)]
        sums = [jnp.zeros((8, SEG), f32) for _ in range(8)]
        for row in range(0, 64, 16):
            rows = slice(row, row + 16)
            vg = st.vg[rows, lanes]
            d_vg = jnp.zeros((16, SEG), f32)
            d = []
            for m in range(9):
                at = slice(64 * m + row, 64 * m + row + 16)
                grad = st.du[at, lanes]
                d_vg = d_vg + grad * st.bm[at, lanes]
                d.append(grad * vg)
            value = st.y[Y_V + row : Y_V + row + 16, lanes]
            gate = st.q[Q_GATE + row : Q_GATE + row + 16, lanes]
            put3(st.dy, D_GATE, 64, row, lanes, value * d_vg)
            st.dv[rows, lanes] = gate * d_vg
            g = [st.g0[64 * m + row : 64 * m + row + 16, lanes] for m in range(4)]
            terms = [g[0] * d[m] for m in range(1, 9)]
            terms[0] = terms[0] + (g[2] * d[3] - g[3] * d[2])
            terms[1] = terms[1] + (g[3] * d[1] - g[1] * d[3])
            terms[2] = terms[2] + (g[1] * d[2] - g[2] * d[1])
            sums = [a + fold(b) for a, b in zip(sums, terms)]
            first = d[0]
            for m in range(1, 9):
                first = first + h[m] * d[m]
            back = [first] + d[1:]
            back[1] = back[1] + (h[3] * d[2] - h[2] * d[3])
            back[2] = back[2] + (h[1] * d[3] - h[3] * d[1])
            back[3] = back[3] + (h[2] * d[1] - h[1] * d[2])
            for m in range(9):
                at = slice(64 * m + row, 64 * m + row + 16)
                high, low = split(back[m])
                st.dg[at, 2 * SEG * i : 2 * SEG * i + SEG] = high
                st.dg[at, 2 * SEG * i + SEG : 2 * SEG * i + 2 * SEG] = low
        d_harm.append([sublane_sum(x) for x in sums])
    d_env = d_env + deactivate(st, dot(c0t[...], st.dy[0:1536, :]), st.sbb, st.dbb, st.dy, D_Z2)
    d_scal = dot(lb0t[...], st.dy[D_Z2 : D_Z2 + 768, :])
    for i, lanes in enumerate(st.segs):
        for row in range(0, 64, 32):
            rows = slice(row, row + 32)
            value = st.y[Y_V + row : Y_V + row + 32, lanes]
            d_value = st.dv[rows, lanes]
            for o in range(3):
                at = slice(64 * o + row, 64 * o + row + 32)
                part = d_scal[at, lanes]
                d_value = d_value + part * st.a0[at, lanes]
                put2(st.wh, st.wl, 128 + 64 * o + row, lanes, value * part)
            put3(st.dy, D_V, 64, row, lanes, d_value)
        hb = st.hb[:, lanes]
        seats = st.sb[0:LANES, lanes]
        seats = jnp.concatenate([seats, seats], axis=1)
        d_gamma = gather_gamma(dot_nt(st.dg[:, 2 * SEG * i : 2 * SEG * i + 2 * SEG], seats))
        d_scale = over_harmonics(st.wh[128:320, lanes], st.wl[128:320, lanes], hb)
        for o in range(3):
            d_gamma = d_gamma + jnp.where(order_mask(o), d_scale[64 * o : 64 * o + 64], 0.0)
        put3(st.dy, D_W0, 64, 0, lanes, with_harmonics(d_gamma, hb))
        gamma = st.gm[i]
        left = [st.gd[len(st.segs) + i], d_gamma]
        left = left + [jnp.where(order_mask(l), gamma, 0.0) for l in range(3)]
        left = jnp.concatenate([jnp.transpose(x) for x in (
            jnp.concatenate(left[0:2], axis=0), jnp.concatenate(left[2:4], axis=0),
            jnp.concatenate([left[4], jnp.zeros((64, LANES), f32)], axis=0),
        )], axis=1)
        high, low = split(left[0:80])
        high, low = high[:, 0:320], low[:, 0:320]
        d_seated = (
            dot(high, st.wh[:, lanes]) + dot(low, st.wh[:, lanes]) + dot(high, st.wl[:, lanes])
        )
        seats = st.sf[:, lanes]
        for m in range(1, 9):
            d_harm[i][m - 1] = d_harm[i][m - 1] + sublane_sum(d_seated[8 * m : 8 * m + 8] * seats)
    d_env = d_env + deactivate(st, dot(cat[...], st.dy[...]), st.sa, st.da, st.a, 0)
    d_basis = dot(e1t[...], st.a[...])[0:8]
    d_env = d_env + read
    dh = [None] + [jnp.concatenate([x[m] for x in d_harm], axis=1) for m in range(8)]
    dux = ROOT3 * dh[1] + ROOT15 * (uy * dh[4] + uz * dh[7] + ux * dh[8]) - ROOT5 * ux * dh[6]
    duy = ROOT3 * dh[2] + ROOT15 * (ux * dh[4] + uz * dh[5] - uy * dh[8]) - ROOT5 * uy * dh[6]
    duz = ROOT3 * dh[3] + ROOT15 * (uy * dh[5] + ux * dh[7]) + 2.0 * ROOT5 * uz * dh[6]
    order = (lax.broadcasted_iota(jnp.int32, (8, st.width), 0) + 1).astype(f32)
    sine_part = sublane_sum(sines * d_basis)
    cos_part = sublane_sum(order * cosines * d_basis)
    d_env = d_env + 0.5 * inv * sine_part
    d_inv = 0.5 * env * sine_part + ox * dux + oy * duy + oz * duz
    d_dist = (math.pi / 8.0) * level * cos_part
    d_sq = -0.125 * ratio * env * env * d_env + 0.5 * inv * d_dist - 0.5 * inv * inv * inv * d_inv
    d_sq = 2.0 * d_sq
    grad = [inv * dux + d_sq * ox, inv * duy + d_sq * oy, inv * duz + d_sq * oz]
    rows = jnp.concatenate(grad + [energy, jnp.zeros((4, st.width), f32)], axis=0)
    for lanes in st.segs:
        high = rows[:, lanes].astype(bf16).astype(f32)
        low = rows[:, lanes] - high
        sent = dot_nt(jnp.concatenate([high, low], axis=0).astype(bf16), st.oh[:, lanes])
        out[...] = out[...] + (sent[0:8] + sent[8:16])


def force_kernel(width, load, mine, other, nbr, *rest):
    sources, outs, tab, names_ref = rest[:10], rest[10:12], rest[12], rest[13]
    raw, weights, full, tall, sems = rest[14:24], rest[24:39], rest[39], rest[40], rest[41]
    total, table, deals, scratch = rest[42], rest[43], rest[44], rest[45:]
    copies = [
        pltpu.make_async_copy(source, target, sems.at[i])
        for i, (source, target) in enumerate(zip(sources, raw))
    ]
    for copy in copies:
        copy.start()
    wide = Stream(scratch, width, width)
    narrow = Stream(scratch, width // 2, width)
    total[...] = jnp.zeros_like(total)
    wide.sb[...] = jnp.zeros_like(wide.sb)
    wide.hb[...] = jnp.zeros_like(wide.hb)
    names_ref[0:16, :] = nbr[...]
    names_ref[16:24, :] = jnp.zeros((8, SEG), jnp.int32)
    names_ref[24:32, :] = other[8:16, :].astype(jnp.int32)
    other_load = jnp.max(other[4:5, 16:17]).astype(jnp.int32)
    segments = deal(load[0], other_load, mine, other, table, deals, sems.at[10])
    kind = lax.broadcasted_iota(jnp.int32, (8, LANES), 0).astype(f32)
    row = lax.broadcasted_iota(jnp.int32, (8, LANES), 0)
    lane = lax.broadcasted_iota(jnp.int32, (8, LANES), 1)
    firsts, seconds = [], []
    for source in (mine, other):
        value = jnp.where(lane < 96, source[0:8, 0:LANES], 0.0)
        place = jnp.where(row < 3, value, 0.0)
        high = place.astype(bf16).astype(f32)
        rest_of = place - high
        mid = rest_of.astype(bf16).astype(f32)
        low = (rest_of - mid).astype(bf16).astype(f32)
        named = (kind == value[3:4]).astype(f32)
        none = jnp.zeros_like(named)
        firsts.append(jnp.concatenate([high, mid, low, none, named, none], axis=0))
        seconds.append(jnp.concatenate([-high, -mid, -low, named, none, none], axis=0)[:, 0:64])
    tab[...] = jnp.concatenate(firsts + [jnp.concatenate(seconds, axis=1)], axis=1).astype(bf16)
    for copy in copies:
        copy.wait()
    prepare_weights(raw, weights, full, tall)
    tiles = lax.shift_right_logical(segments + 1, 2)

    def step(at, carry):
        tile(wide, weights, deals, tab, names_ref, total, at * 4)
        return carry

    lax.fori_loop(0, tiles, step, 0)

    @pl.when(segments > tiles * 4)
    def _():
        tile(narrow, weights, deals, tab, names_ref, total, tiles * 4)

    none = jnp.zeros((8, 64), f32)
    for owner in range(2):
        start = 2 * LANES + 64 * owner
        centers = jnp.concatenate([total[:, start : start + 64], none], axis=1)
        names = total[:, LANES * owner : LANES * owner + LANES]
        outs[owner][...] = jnp.where(row < 3, centers - names, centers)


def run_forces(load, mine, other, nbr, weights, width=1024):
    scratch = scratch_list(width)
    vmem = pl.BlockSpec(memory_space=pltpu.VMEM)
    smem = pl.BlockSpec(memory_space=pltpu.SMEM)
    return pl.pallas_call(
        functools.partial(force_kernel, width),
        out_shape=[jax.ShapeDtypeStruct((8, LANES), f32)] * 2,
        in_specs=[smem] + [vmem] * 3 + [pl.BlockSpec(memory_space=pl.ANY)] * len(weights),
        out_specs=[vmem, vmem],
        scratch_shapes=[pltpu.VMEM((48, 384), bf16), pltpu.VMEM((32, SEG), jnp.int32)]
        + [pltpu.VMEM(shape, f32) for shape in RAW_SHAPES]
        + [pltpu.VMEM(shape, bf16) for shape in READY_SHAPES]
        + [pltpu.VMEM((128, LANES), f32), pltpu.VMEM((896, 256), f32)]
        + [pltpu.VMEM((D_ALL, 256), f32), pltpu.SemaphoreType.DMA((len(weights) + 1,))]
        + [pltpu.VMEM((8, 384), f32), pltpu.VMEM((8, LANES), jnp.int32)]
        + [pltpu.SMEM((8, LANES), jnp.int32)]
        + [pltpu.VMEM(shape, kind) for shape, kind in scratch.values()],
        compiler_params=pltpu.CompilerParams(vmem_limit_bytes=FORCES_MIB * 2**20),
        name="forces",
    )(load, mine, other, nbr, *weights)


def shell_kernel(ghost, place, kind, out):
    lane = lax.broadcasted_iota(jnp.int32, (8, 64), 1)
    whole = jnp.concatenate([place[...], kind[...].astype(f32), jnp.zeros((4, 64), f32)], axis=0)
    spot = lax.broadcasted_iota(jnp.int32, (8, 8), 1)
    total = jnp.zeros((8, 8), f32)
    for k in range(8):
        one = jnp.sum(jnp.where(lane == ghost[k], whole, 0.0), axis=1, keepdims=True)
        total = total + jnp.where(spot == k, one, 0.0)
    out[...] = total[0:4]


def shell_of(ghost, place, kind):
    vmem = pl.BlockSpec(memory_space=pltpu.VMEM)
    return pl.pallas_call(
        shell_kernel,
        out_shape=jax.ShapeDtypeStruct((4, 8), f32),
        in_specs=[pl.BlockSpec(memory_space=pltpu.SMEM), vmem, vmem],
        out_specs=vmem,
        name="shell",
    )(ghost, place, kind[None])


def payload_kernel(load, place, kind, first, second, third, fourth, counts, nbr, out):
    whole = jnp.concatenate([place[...], kind[...].astype(f32)], axis=0)
    top = jnp.concatenate(
        [whole, first[...], second[...], third[...], fourth[...], jnp.zeros((4, 160), f32)], axis=1
    )
    loads = jnp.zeros((4, 1), jnp.int32) + load[0]
    low = jnp.concatenate(
        [counts[...].astype(f32), loads.astype(f32), jnp.zeros((4, SEG - 17), f32)], axis=1
    )
    out[0:8, :] = jnp.concatenate([top, low], axis=0)
    out[8:16, :] = nbr[8:16, :].astype(f32)


def payload_of(load, place, kind, shells, counts, nbr):
    vmem = pl.BlockSpec(memory_space=pltpu.VMEM)
    return pl.pallas_call(
        payload_kernel,
        out_shape=jax.ShapeDtypeStruct((16, SEG), f32),
        in_specs=[pl.BlockSpec(memory_space=pltpu.SMEM)] + [vmem] * 8,
        out_specs=vmem,
        name="payload",
    )(load, place, kind[None], *shells, counts, nbr)


def all_weights(w_embed1, w_embed2, w_v0, w_env, w_lat1, w_lat2, w_gate, w_mix, w_out1, w_out2):
    return (
        w_embed1.T, w_embed2, w_v0, w_env, jnp.swapaxes(w_lat1, 1, 2), w_lat2, w_gate, w_mix,
        w_out1, w_out2[None],
    )


def beside(cells, axis, step):
    count = lax.axis_size(axis)
    return lax.ppermute(cells, axis, [(i, (i + step) % count) for i in range(count)])


def helper(cells):
    count = lax.axis_size("dom")
    return lax.ppermute(cells, "dom", [(i, i ^ 8) for i in range(count)])


def local(
    positions,
    species,
    ghost_index,
    bin_load,
    neighbour,
    pair_count,
    species_shift,
    w_embed1,
    w_embed2,
    w_v0,
    w_env,
    w_lat1,
    w_lat2,
    w_gate,
    w_mix,
    w_out1,
    w_out2,
):
    atoms = positions.shape[1]
    centers = pair_count.shape[1]
    ghosts = ghost_index.shape[0]
    load = bin_load[0]
    named = ghost_index[:, None] == jnp.arange(atoms)[None, :]
    counts = pair_count.T
    shell = shell_of(ghost_index, positions, species)
    received = [beside(shell, "grp", 1), beside(shell, "grp", -1), beside(shell, "dom", 1), beside(shell, "dom", -1)]
    weights = all_weights(
        w_embed1, w_embed2, w_v0, w_env, w_lat1, w_lat2, w_gate, w_mix, w_out1, w_out2
    )
    mine = payload_of(bin_load, positions, species, received, counts, neighbour)
    other = helper(mine)
    result, helped = run_forces(bin_load, mine, other, neighbour, weights)
    result = result + helper(helped)
    energies = result[3, :atoms]
    force = result[0:3, :atoms]
    ghost = result[0:3, atoms : atoms + 4 * ghosts].reshape(3, 4, ghosts)
    back = (
        beside(ghost[:, 0], "grp", -1)
        + beside(ghost[:, 1], "grp", 1)
        + beside(ghost[:, 2], "dom", -1)
        + beside(ghost[:, 3], "dom", 1)
    )
    forces = force + jnp.sum(jnp.where(named[None], back[:, :, None], 0.0), axis=1)
    live = jnp.arange(atoms) // centers < load
    kind_range = jnp.arange(species_shift.shape[0])
    shift = jnp.sum(
        jnp.where(species[:, None] == kind_range[None], species_shift[None, :], 0.0), axis=1
    )
    return (forces, energies + jnp.where(live, shift, 0.0))


def solution(mesh):
    spread_over = ("grp", "dom")
    in_specs = (
        P(None, spread_over),
        P(spread_over),
        P(spread_over),
        P(spread_over),
        P(spread_over, None),
        P(spread_over, None),
    ) + (P(),) * 11
    out_specs = (P(None, spread_over), P(spread_over))
    return jax.shard_map(local, mesh=mesh, in_specs=in_specs, out_specs=out_specs, check_vma=False)
```
